512 devices in a mesh: seq: 64 (over z_lo, y, core), dp: 8 (over z_hi, x).
Axes of the slice: x: 4, y: 8, z: 8 (z_hi: 2, z_lo: 4; z = z_hi * 4 + z_lo), core: 2. Of those that a mesh axis runs over, the one named last changes fastest.
Arguments:
- sequence_acts: bfloat16 [8, 768, 16384], P('dp', None, 'seq'), may hold values from -6 to 6
- taps: float32 [2, 768, 3], replicated, may hold values from -2.5 to 2.5
- dilations: int32 [2], replicated, may hold values from 1 to 8, as said below
- left_link: int32 [8, 64], P('dp'), may hold values from -1 to 63, as said below
- projection: bfloat16 [896, 768], P('dp'), may hold values from -0.21875 to 0.21875
- head_cotangent: bfloat16 [8, 896, 8192], P('dp', 'seq'), may hold values from -16 to 16
Outputs:
- input_grad: bfloat16 [8, 768, 16384], P('dp', None, 'seq')
- projection_grad: float32 [896, 768], P('seq')
- taps_grad: float32 [2, 768, 3], replicated
The draws below stay inside these ranges and needn't reach their ends.
Inputs may be any that keep to these rules, and one draw needn't show every extreme that they name: `dilations`: the last block's dilation is 8. `left_link`: entry s is -1 or (s - 1) mod 64; entry 0 is never -1; each window has at least one -1.
All inputs are finite; a program needn't handle non-finite values.
Results may differ from the reference program's by a relative error of at most 0.0058.
Values may be sent and summed in bfloat16 or wider, within the bound.
A program may use at most 64 MiB of HBM per device.

```python
import math
import jax
import jax.numpy as jnp
from jax import lax

C = 768
OUT_C = 896
DEVICE_ROWS = 256
BLOCK_COUNT = 2
DILATION_LIMIT = 8
SAMPLES = 8
LENGTH = 16384
POOLED = 8192
N_SEQ = 64


def draw_dilations(key, part):
    key = jax.random.fold_in(key, 11)
    input_values = jax.random.randint(key, (BLOCK_COUNT,), 1, DILATION_LIMIT + 1)
    final_block = jnp.arange(BLOCK_COUNT) == BLOCK_COUNT - 1
    return jnp.where(final_block, DILATION_LIMIT, input_values).astype(jnp.int32)


def draw_left_link(key, part):
    key = jax.random.fold_in(key, 23)
    start_key, break_key = jax.random.split(key)
    start_offset = jax.random.randint(start_key, (SAMPLES, 1), 1, N_SEQ)
    breaks = jax.random.randint(break_key, (SAMPLES, N_SEQ), 0, 4) == 0
    shard = jnp.arange(N_SEQ)[None, :]
    before = (shard - 1) % N_SEQ
    cut = (shard == start_offset) | breaks & (shard != 0)
    return jnp.where(cut, -1, before).astype(jnp.int32)


def with_spikes(array, stream_key, source, target, parts, factor):
    owner, partner = [(jnp.arange(array.shape[dim]) // (array.shape[dim] // parts)).reshape([-1 if axis == dim else 1 for axis in range(array.ndim)]) for dim in (source, target)]
    chosen = jax.random.permutation(stream_key, parts)[partner]
    strong = (owner == chosen) | (owner == (partner + parts // 2) % parts)
    return jnp.where(strong, factor * array, array)


def block_scale(own_key, extent, pieces, smallest, largest):
    loudness = 1.0
    for position, parts in pieces:
        steps = jax.random.uniform(jax.random.fold_in(jax.random.fold_in(own_key, 6), position), (parts,), jnp.float32, smallest / len(pieces), largest / len(pieces))
        loudness = loudness * jnp.repeat(jnp.exp(steps), extent[position] // parts).reshape((-1,) + (1,) * (len(extent) - 1 - position))
    return loudness


def scatter_about(key, extent, deviation, reach, shards=(), kind=jnp.bfloat16):
    values = jax.random.normal(key, extent, jnp.float32) * deviation
    if len(shards) > 0:
        values = block_scale(key, extent, shards, -0.22, 0.18) * values
    return jnp.clip(values, min=-reach, max=reach).astype(kind)


def heavy_noise(rng, shape, width, limit, shards, heavy, kind=jnp.bfloat16):
    values = width * jax.random.normal(rng, shape, jnp.float32)
    if shards:
        values = values * block_scale(rng, shape, shards, -0.22, 0.18)
    return jnp.clip(with_spikes(values, jax.random.fold_in(rng, 3), *heavy), -limit, limit).astype(kind)


def setup_inputs(seed: int = 0) -> dict:
    arg_keys = jax.random.split(jax.random.key(seed), 7)
    return {
        "sequence_acts": scatter_about(arg_keys[0], (SAMPLES, C, LENGTH), 1.0, 6.0, ((0, 8), (2, 64))),
        "taps": scatter_about(arg_keys[1], (BLOCK_COUNT, C, 3), 0.4, 2.5, (), jnp.float32),
        "dilations": draw_dilations(jax.random.fold_in(arg_keys[6], 71), 0),
        "left_link": draw_left_link(jax.random.fold_in(arg_keys[6], 71), 0),
        "projection": scatter_about(arg_keys[4], (OUT_C, C), C ** -0.5, 0.21875, ((0, 8),)),
        "head_cotangent": heavy_noise(arg_keys[5], (SAMPLES, OUT_C, POOLED), 1.0, 16.0, ((0, 8), (1, 64)), (2, 1, 64, 4.0)),
    }


gelu_scale = 0.7978845608028654

def gelu_result(v):
    inner = jnp.tanh(gelu_scale * (v + 0.044715 * v * v * v))
    return 0.5 * v * (1.0 + inner)

def gelu_slope(v):
    inner = jnp.tanh(gelu_scale * (v + 0.044715 * v * v * v))
    return 0.5 * (1.0 + inner) + 0.5 * v * (1.0 - inner * inner) * gelu_scale * (1.0 + 3.0 * 0.044715 * v * v)

def with_rims(block_params, link):
    left_linked = link >= 0
    right_linked = jnp.roll(left_linked, -1)
    left_border = jnp.roll(block_params[:, :, DEVICE_ROWS - DILATION_LIMIT:], 1, axis=1)
    right_border = jnp.roll(block_params[:, :, :DILATION_LIMIT], -1, axis=1)
    left_border = jnp.where(left_linked[None, :, None], left_border, jnp.zeros_like(left_border))
    right_border = jnp.where(right_linked[None, :, None], right_border, jnp.zeros_like(right_border))
    return jnp.concatenate([left_border, block_params, right_border], axis=2)

def tap_sum(extended_rows, weights, dilation, length, sign):
    margin = (extended_rows.shape[2] - length) // 2
    total = jnp.zeros((extended_rows.shape[0], extended_rows.shape[1], length), jnp.float32)
    for tap_index in range(3):
        start_offset = (margin + sign * (tap_index - 1) * dilation).astype(jnp.int32)
        total = total + weights[:, tap_index][:, None, None] * lax.dynamic_slice_in_dim(extended_rows, start_offset, length, 2)
    return total

def one_window(sequence, link, cotangent, taps, dilations, projection):
    running_state = sequence.reshape(C, N_SEQ, DEVICE_ROWS)
    inputs = []
    acts = []
    for block_number in range(BLOCK_COUNT):
        inputs.append(running_state)
        block_activation = gelu_result(with_rims(running_state, link).astype(jnp.float32))
        acts.append(block_activation)
        mixed = tap_sum(block_activation, taps[block_number], dilations[block_number], DEVICE_ROWS, 1)
        running_state = (running_state.astype(jnp.float32) + mixed).astype(jnp.bfloat16)
    pooled = (0.5 * (running_state[:, :, 0::2].astype(jnp.float32) + running_state[:, :, 1::2].astype(jnp.float32))).astype(jnp.bfloat16)
    pooled = pooled.reshape(C, POOLED)
    back_pool = jnp.dot(projection.T, cotangent, preferred_element_type=jnp.float32)
    running_gradient = (0.5 * back_pool).astype(jnp.bfloat16).reshape(C, N_SEQ, DEVICE_ROWS // 2)
    running_gradient = jnp.repeat(running_gradient, 2, axis=2)
    tap_grads = [None] * BLOCK_COUNT
    for block_number in reversed(range(BLOCK_COUNT)):
        extended_rows = with_rims(running_gradient, link).astype(jnp.float32)
        back = tap_sum(extended_rows, taps[block_number], dilations[block_number], DEVICE_ROWS, -1)
        grad_f = running_gradient.astype(jnp.float32)
        columns = []
        for tap_index in range(3):
            start_offset = (DILATION_LIMIT + (tap_index - 1) * dilations[block_number]).astype(jnp.int32)
            shifted = lax.dynamic_slice_in_dim(acts[block_number], start_offset, DEVICE_ROWS, 2)
            columns.append(lax.optimization_barrier(jnp.sum(grad_f * shifted, axis=(1, 2))))
        tap_grads[block_number] = jnp.stack(columns, axis=1)
        running_gradient = (grad_f + back * gelu_slope(inputs[block_number].astype(jnp.float32))).astype(jnp.bfloat16)
    weight_grad = jnp.dot(cotangent, pooled.T, preferred_element_type=jnp.float32)
    return (running_gradient.reshape(C, LENGTH), weight_grad, jnp.stack(tap_grads, axis=0))

def reference(sequence_acts, taps, dilations, left_link, projection, head_cotangent):

    def step(index):
        return one_window(sequence_acts[index], left_link[index], head_cotangent[index], taps, dilations, projection)
    grads, weight_grads, tap_grads = lax.map(step, jnp.arange(SAMPLES, dtype=jnp.int32))
    scale = 1.0 / math.sqrt(SAMPLES * POOLED)
    return (grads, lax.optimization_barrier(jnp.sum(weight_grads, axis=0)) * scale, lax.optimization_barrier(jnp.sum(tap_grads, axis=0)) * scale)
```

```python
import functools
import math

import jax
import jax.numpy as jnp
from jax import lax
from jax.experimental import pallas as pl
from jax.experimental.pallas import tpu as pltpu
from jax.sharding import PartitionSpec as P

MESH = pl.DeviceIdType.MESH
BF = jnp.bfloat16
F32 = jnp.float32

C = 768
ROWS = 256
HALF = 128
SEQ = 64
DP = 8
OWN = 14
PAD = 16
SLAB = 32
LAST_DILATION = 8
GELU = 0.7978845608028654


def gelu_pair(v):
    th = jnp.tanh(GELU * (v + 0.044715 * v * v * v))
    act = 0.5 * v * (1.0 + th)
    slope = 0.5 * (1.0 + th) + 0.5 * v * (1.0 - th * th) * GELU * (1.0 + 3.0 * 0.044715 * v * v)
    return act, slope


def rounded(v):
    return v.astype(BF).astype(F32)


def earlier(tiles, lane, d):
    turned = [pltpu.roll(t, d, 1) for t in tiles]
    return [jnp.where(lane < d, turned[j - 1], turned[j]) for j in range(len(tiles))]


def later(tiles, lane, d):
    turned = [pltpu.roll(t, HALF - d, 1) for t in tiles]
    n = len(tiles)
    return [jnp.where(lane >= HALF - d, turned[(j + 1) % n], turned[j]) for j in range(n)]


def kernel(
    x_ref, taps_ref, dil_ref, link_ref, proj_ref, cot_ref,
    out_ref, pg_ref, tg_ref,
    stage, cot, cot_sib, pfull, edge_s, edge_r, gedge_s, gedge_r, halo, wcol,
    a0, a1, s0, s1, x2, pooled, pooled_sib, g2, tcol,
    a_s1, a_r1, a_s2, a_r2, a_s3, a_r3, a_r4, b_s1, b_r1, b_s2, b_r2, b_r3,
    t_s, t_r1, t_r2, t_r3, t_f,
    send, recv,
):
    s = lax.axis_index("seq")
    d = lax.axis_index("dp")
    core = s % 2
    y = (s // 2) % 8
    zl = s // 16
    x = d % 4
    zh = d // 4
    z8 = zh * 4 + zl
    sib = s + 1 - 2 * core

    def at_x(k):
        return {"seq": s, "dp": zh * 4 + (x + k) % 4}

    def at_x_core(xx, cc):
        return {"seq": s - core + cc, "dp": zh * 4 + xx}

    def at_y(yy):
        return {"seq": zl * 16 + yy * 2 + core, "dp": d}

    def at_z(zz):
        return {"seq": (zz % 4) * 16 + y * 2 + core, "dp": (zz // 4) * 4 + x}

    def push(src, dst, i, where):
        pltpu.make_async_remote_copy(
            src_ref=src, dst_ref=dst, send_sem=send.at[i], recv_sem=recv.at[i],
            device_id=where, device_id_type=MESH,
        ).start()

    def dummy(ref, i):
        return pltpu.make_async_remote_copy(
            src_ref=ref, dst_ref=ref, send_sem=send.at[i], recv_sem=recv.at[i],
            device_id={"seq": sib, "dp": d}, device_id_type=MESH,
        )

    def arrived(ref, i):
        dummy(ref, i).wait_recv()

    def sent(ref, i):
        dummy(ref, i).wait_send()

    barrier = pltpu.get_barrier_semaphore()

    def greet(where):
        pl.semaphore_signal(barrier, inc=1, device_id=where, device_id_type=MESH)

    @pl.loop(1, SEQ)
    def _(k):
        greet({"seq": (s + k) % SEQ, "dp": d})

    for k in range(4):
        greet({"seq": ((zl + k) % 4) * 16 + y * 2 + core, "dp": (1 - zh) * 4 + x})
    for k in range(1, 4):
        greet(at_x(k))
        greet({"seq": sib, "dp": zh * 4 + (x + k) % 4})

    lane = lax.broadcasted_iota(jnp.int32, (1, HALF), 1)

    def pack_edges(read, dst):
        for side in range(2):
            total = None
            for k in range(8):
                rows = pl.ds(96 * k, 96)
                part = read(1 - side, rows).astype(F32)
                part = pltpu.roll(part, (16 * k + 16 * (1 - side)) % HALF, 1)
                keep = (lane >= 16 * k) & (lane < 16 * k + 16)
                total = jnp.where(keep, part, 0.0 if total is None else total)
            dst[side] = total.astype(BF)

    left_linked = link_ref[0, s] >= 0
    right_linked = link_ref[0, (s + 1) % SEQ] >= 0

    def halo_keep(width):
        return ((lane < width) & right_linked) | ((lane >= HALF - width) & left_linked)

    def unpack_edges(src, dst):
        from_left = src[0].astype(F32)
        from_right = src[1].astype(F32)
        for k in range(8):
            left = pltpu.roll(from_left, (HALF - 16 - 16 * k) % HALF, 1)
            right = pltpu.roll(from_right, (HALF - 16 * k) % HALF, 1)
            tile = jnp.where(lane < HALF // 2, right, left)
            dst[pl.ds(96 * k, 96), :] = jnp.where(halo_keep(16), tile, 0.0)

    pack_edges(lambda j, rows: x_ref[0, rows, pl.ds(HALF * j, HALF)], edge_s)

    for t in range(SEQ):
        block = cot_ref[0, :, pl.ds(HALF * t, HALF)]
        stage[t] = jnp.concatenate(
            [block.astype(F32), jnp.zeros((PAD - OWN, HALF), F32)], axis=0
        ).astype(BF)

    row = lax.broadcasted_iota(jnp.int32, (HALF, 112), 0)
    col = lax.broadcasted_iota(jnp.int32, (HALF, 112), 1)
    inner = row % PAD
    source = OWN * (2 * ((row // PAD) % 4) + row // 64) + inner
    pick = jnp.where((inner < OWN) & (source == col), 1.0, 0.0).astype(BF)
    own_rows = jnp.dot(pick, proj_ref[...], preferred_element_type=F32).astype(BF)
    pfull[0, d] = own_rows[:64]
    pfull[1, d] = own_rows[64:]

    pl.semaphore_wait(barrier, SEQ - 1 + 4 + 6)

    push(edge_s.at[0], edge_r.at[0], 0, {"seq": (s + 1) % SEQ, "dp": d})
    push(edge_s.at[1], edge_r.at[1], 1, {"seq": (s + SEQ - 1) % SEQ, "dp": d})
    partner = {"seq": s, "dp": (1 - zh) * 4 + x}
    push(pfull.at[core, d], pfull.at[core, d], 2, partner)
    for k in (1, 3, 2):
        push(pfull.at[core, d], pfull.at[core, d], 2 + k, at_x(k))
    me = core * 32 + zl * 8 + y
    @pl.loop(1, SEQ)
    def _(k):
        t = (s + k) % SEQ
        push(stage.at[t], cot.at[me], 6, {"seq": t, "dp": d})

    cot[me] = stage[s]

    six = jnp.concatenate([taps_ref[k] for k in range(3)] + [jnp.zeros((2, C), F32)], axis=0)
    wcol[...] = jnp.transpose(six)
    d0 = dil_ref[0]

    def weights(rows):
        return [[wcol[rows, 2 * k + b:2 * k + b + 1] for k in range(3)] for b in range(2)]

    arrived(edge_r.at[0], 0)
    arrived(edge_r.at[1], 1)
    unpack_edges(edge_r, halo)

    @pl.loop(0, C // SLAB)
    def _(i):
        rows = pl.ds(pl.multiple_of(i * SLAB, SLAB), SLAB)
        w = weights(rows)
        xs = [x_ref[0, rows, :HALF].astype(F32), x_ref[0, rows, HALF:].astype(F32), halo[rows, :]]
        acts = []
        for j in range(3):
            act, slope = gelu_pair(xs[j])
            acts.append(act)
            a0[j, rows, :] = act
            if j < 2:
                s0[j, rows, :] = slope
        lo, hi = earlier(acts, lane, d0), later(acts, lane, d0)
        ones = []
        acts1 = []
        for j in range(3):
            v = rounded(xs[j] + ((w[0][0] * lo[j] + w[0][1] * acts[j]) + w[0][2] * hi[j]))
            if j == 2:
                v = jnp.where(halo_keep(8), v, 0.0)
            ones.append(v)
            act, slope = gelu_pair(v)
            acts1.append(act)
            a1[j, rows, :] = act
            s1[j, rows, :] = slope
        lo, hi = earlier(acts1, lane, LAST_DILATION), later(acts1, lane, LAST_DILATION)
        for j in range(2):
            v = ones[j] + ((w[1][0] * lo[j] + w[1][1] * acts1[j]) + w[1][2] * hi[j])
            x2[rows, HALF * j:HALF * (j + 1)] = v.astype(BF)

    two = lax.broadcasted_iota(jnp.int32, (ROWS, HALF), 0) // 2
    pair = two == lax.broadcasted_iota(jnp.int32, (ROWS, HALF), 1)
    halves = jnp.where(pair, 0.5, 0.0).astype(BF)
    pooled[...] = jnp.dot(x2[...], halves, preferred_element_type=F32).astype(BF)
    push(pooled, pooled_sib, 7, {"seq": sib, "dp": d})

    other = (1 - zh) * 4 + x
    sibling = {"seq": sib, "dp": d}
    arrived(pfull.at[core, other], 2)
    for k in (1, 3, 2):
        push(pfull.at[core, other], pfull.at[core, other], 7 + k, at_x(k))
    push(pfull.at[core, other], pfull.at[core, other], 11, sibling)

    arrived(cot.at[pl.ds(0, SEQ - 1)], 6)
    push(cot.at[pl.ds((1 - core) * 32, 32)], cot_sib, 12, sibling)
    arrived(pooled_sib, 7)
    arrived(cot_sib, 12)
    mine = cot[pl.ds(core * 32, 32)].reshape(512, HALF)
    theirs = cot_sib[...].reshape(512, HALF)
    nt = (((1,), (1,)), ((), ()))
    for j in (2, 0, 1):
        cols = pl.ds(256 * j, 256)
        part = lax.dot_general(mine, pooled[cols, :], nt, preferred_element_type=F32)
        part = part + lax.dot_general(theirs, pooled_sib[cols, :], nt, preferred_element_type=F32)
        part = part.astype(BF)
        if j == 2:
            b_s1[...] = part.reshape(4, 8, PAD, 256)
            @pl.loop(1, 8)
            def _(k):
                yy = (y + k) % 8
                push(b_s1.at[:, yy], b_r1.at[y], 13, at_y(yy))
        else:
            a_s1[2 * j] = part[:, :HALF].reshape(4, 8, PAD, HALF)
            a_s1[2 * j + 1] = part[:, HALF:].reshape(4, 8, PAD, HALF)
    for k in (1, 3, 2):
        push(a_s1.at[(x + k) % 4], a_r1.at[x], 14, at_x(k))
    b_r1[y] = b_s1[:, y]
    a_r1[x] = a_s1[x]

    for k in (1, 3, 2):
        arrived(pfull.at[core, d], 2 + k)
        blk = zh * 4 + (x + 4 - k) % 4
        push(pfull.at[core, blk], pfull.at[core, blk], 14 + k, sibling)
    for k in (1, 3, 2):
        arrived(pfull.at[core, d], 7 + k)
        blk = (1 - zh) * 4 + (x + 4 - k) % 4
        push(pfull.at[core, blk], pfull.at[core, blk], 17 + k, sibling)
    arrived(pfull.at[core, d], 11)
    for k in (1, 2, 3):
        arrived(pfull.at[core, d], 14 + k)
        arrived(pfull.at[core, d], 17 + k)
    back = lax.dot_general(
        cot[...].reshape(SEQ * PAD, HALF), pfull[...].reshape(SEQ * PAD, C),
        (((0,), (0,)), ((), ())), preferred_element_type=F32,
    )
    back = (0.5 * back).astype(BF)
    two = lax.broadcasted_iota(jnp.int32, (HALF, ROWS), 1) // 2
    spread = jnp.where(two == lax.broadcasted_iota(jnp.int32, (HALF, ROWS), 0), 1.0, 0.0).astype(BF)
    g2[...] = lax.dot_general(back, spread, (((0,), (0,)), ((), ())), preferred_element_type=F32)
    pack_edges(lambda j, rows: g2[rows, HALF * j:HALF * (j + 1)], gedge_s)
    push(gedge_s.at[0], gedge_r.at[0], 21, {"seq": (s + 1) % SEQ, "dp": d})
    push(gedge_s.at[1], gedge_r.at[1], 22, {"seq": (s + SEQ - 1) % SEQ, "dp": d})
    arrived(gedge_r.at[0], 21)
    arrived(gedge_r.at[1], 22)
    unpack_edges(gedge_r, halo)

    @pl.loop(0, C // SLAB)
    def _(i):
        rows = pl.ds(pl.multiple_of(i * SLAB, SLAB), SLAB)
        w = weights(rows)
        cols = jnp.zeros((SLAB, HALF), F32)

        def tap_columns(cols, g, a, dist, b):
            shifted = (earlier(a, lane, dist), a, later(a, lane, dist))
            for k in range(3):
                total = jnp.sum(g[0] * shifted[k][0] + g[1] * shifted[k][1], axis=1, keepdims=True)
                cols = jnp.where(lane == 2 * k + b, total, cols)
            return cols

        g = [g2[rows, :HALF], g2[rows, HALF:], halo[rows, :]]
        cols = tap_columns(cols, g, [a1[j, rows, :] for j in range(3)], LAST_DILATION, 1)
        lo, hi = earlier(g, lane, LAST_DILATION), later(g, lane, LAST_DILATION)
        g1 = []
        for j in range(3):
            conv = (w[1][0] * hi[j] + w[1][1] * g[j]) + w[1][2] * lo[j]
            g1.append(rounded(g[j] + conv * s1[j, rows, :]))
        g1[2] = jnp.where(halo_keep(8), g1[2], 0.0)
        cols = tap_columns(cols, g1, [a0[j, rows, :] for j in range(3)], d0, 0)
        lo, hi = earlier(g1, lane, d0), later(g1, lane, d0)
        for j in range(2):
            conv = (w[0][0] * hi[j] + w[0][1] * g1[j]) + w[0][2] * lo[j]
            out_ref[0, rows, HALF * j:HALF * (j + 1)] = (g1[j] + conv * s0[j, rows, :]).astype(BF)
        tcol[rows, :] = cols

    flat = jnp.transpose(tcol[...])[:8]
    t_s[0] = flat[:, :384]
    t_s[1] = flat[:, 384:]
    slot = x * 2 + core
    t_r1[slot] = t_s[core]
    for k in range(4):
        for c in range(2):
            cc = (core + c) % 2
            if k or c:
                push(t_s.at[cc], t_r1.at[slot], 23, at_x_core((x + k) % 4, cc))

    def total(ref):
        parts = [ref[i].astype(F32) for i in range(ref.shape[0])]
        while len(parts) > 1:
            parts = [a + b for a, b in zip(parts[::2], parts[1::2])]
        return parts[0]

    arrived(b_r1.at[pl.ds(0, 7)], 13)
    b_s2[...] = total(b_r1).astype(BF)
    @pl.loop(1, 8)
    def _(k):
        zz = (z8 + k) % 8
        push(b_s2.at[zz % 4], b_r2.at[z8], 24, at_z(zz))
    b_r2[z8] = b_s2[zl]

    arrived(a_r1.at[pl.ds(0, 3)], 14)
    a_s2[...] = total(a_r1).astype(BF)
    @pl.loop(1, 8)
    def _(k):
        yy = (y + k) % 8
        push(a_s2.at[:, yy], a_r2.at[y], 25, at_y(yy))
    a_r2[y] = a_s2[:, y]

    arrived(t_r1.at[pl.ds(0, 7)], 23)
    t_r2[y] = total(t_r1)
    @pl.loop(1, 8)
    def _(k):
        push(t_r2.at[y], t_r2.at[y], 26, at_y((y + k) % 8))

    arrived(b_r2.at[pl.ds(0, 7)], 24)
    b_r3[x] = total(b_r2)
    for k in (1, 3, 2):
        push(b_r3.at[x], b_r3.at[x], 27, at_x(k))

    arrived(a_r2.at[pl.ds(0, 7)], 25)
    a_s3[...] = total(a_r2).astype(BF)
    @pl.loop(1, 8)
    def _(k):
        zz = (z8 + k) % 8
        push(a_s3.at[zz % 4], a_r3.at[z8], 28, at_z(zz))
    a_r3[z8] = a_s3[zl]

    arrived(t_r2.at[pl.ds(0, 7)], 26)
    t_r3[z8] = total(t_r2)
    @pl.loop(1, 8)
    def _(k):
        push(t_r3.at[z8], t_r3.at[z8], 29, at_z((z8 + k) % 8))

    arrived(a_r3.at[pl.ds(0, 7)], 28)
    a_r4[x] = total(a_r3)
    for k in (1, 3, 2):
        push(a_r4.at[x], a_r4.at[x], 30, at_x(k))

    arrived(t_r3.at[pl.ds(0, 7)], 29)
    t_f[core] = total(t_r3)
    push(t_f.at[core], t_f.at[core], 31, sibling)

    scale = 1.0 / math.sqrt(SEQ * DP * HALF)
    arrived(b_r3.at[pl.ds(0, 3)], 27)
    pg_ref[:, 512:] = total(b_r3)[:OWN] * scale
    arrived(a_r4.at[pl.ds(0, 3)], 30)
    for j in range(4):
        pg_ref[:, HALF * j:HALF * (j + 1)] = a_r4[j][:OWN] * scale
    arrived(t_f.at[core], 31)
    for h in range(2):
        for k in range(3):
            tg_ref[k, :, 384 * h:384 * (h + 1)] = t_f[h][2 * k:2 * k + 2] * scale

    sent(edge_s.at[0], 0)
    sent(edge_s.at[1], 1)
    for i in range(2, 6):
        sent(pfull.at[0, 0], i)
    sent(stage.at[pl.ds(0, SEQ - 1)], 6)
    sent(pooled, 7)
    for i in (8, 9, 10, 11, 15, 16, 17, 18, 19, 20):
        sent(pfull.at[0, 0], i)
    sent(cot_sib, 12)
    sent(b_r1.at[pl.ds(0, 7)], 13)
    sent(a_r1.at[pl.ds(0, 3)], 14)
    sent(gedge_s.at[0], 21)
    sent(gedge_s.at[1], 22)
    sent(t_r1.at[pl.ds(0, 7)], 23)
    sent(b_r2.at[pl.ds(0, 7)], 24)
    sent(a_r2.at[pl.ds(0, 7)], 25)
    sent(t_r2.at[pl.ds(0, 7)], 26)
    sent(b_r3.at[pl.ds(0, 3)], 27)
    sent(a_r3.at[pl.ds(0, 7)], 28)
    sent(t_r3.at[pl.ds(0, 7)], 29)
    sent(a_r4.at[pl.ds(0, 3)], 30)
    sent(t_f.at[0], 31)


SCRATCH = [
    ((SEQ, PAD, HALF), BF),
    ((SEQ, PAD, HALF), BF),
    ((32, PAD, HALF), BF),
    ((2, DP, 64, C), BF),
    ((2, 96, HALF), BF),
    ((2, 96, HALF), BF),
    ((2, 96, HALF), BF),
    ((2, 96, HALF), BF),
    ((C, HALF), F32),
    ((C, 8), F32),
    ((3, C, HALF), F32),
    ((3, C, HALF), F32),
    ((2, C, HALF), F32),
    ((3, C, HALF), F32),
    ((C, ROWS), BF),
    ((C, HALF), BF),
    ((C, HALF), BF),
    ((C, ROWS), F32),
    ((C, HALF), F32),
    ((4, 4, 8, PAD, HALF), BF),
    ((4, 4, 8, PAD, HALF), BF),
    ((4, 8, PAD, HALF), BF),
    ((8, 4, PAD, HALF), BF),
    ((4, PAD, HALF), BF),
    ((8, PAD, HALF), BF),
    ((4, PAD, HALF), F32),
    ((4, 8, PAD, 256), BF),
    ((8, 4, PAD, 256), BF),
    ((4, PAD, 256), BF),
    ((8, PAD, 256), BF),
    ((4, PAD, 256), F32),
    ((2, 8, 384), F32),
    ((8, 8, 384), F32),
    ((8, 8, 384), F32),
    ((8, 8, 384), F32),
    ((2, 8, 384), F32),
]


def local(sequence_acts, taps, dilations, left_link, projection, head_cotangent):
    vmem = pl.BlockSpec(memory_space=pltpu.VMEM)
    smem = pl.BlockSpec(memory_space=pltpu.SMEM)
    grad, weight, tap_grads = pl.pallas_call(
        kernel,
        out_shape=(
            jax.ShapeDtypeStruct((1, C, ROWS), BF),
            jax.ShapeDtypeStruct((OWN, C), F32),
            jax.ShapeDtypeStruct((3, 2, C), F32),
        ),
        in_specs=[vmem, vmem, smem, smem, vmem, vmem],
        out_specs=(vmem, vmem, vmem),
        scratch_shapes=[pltpu.VMEM(shape, kind) for shape, kind in SCRATCH]
        + [pltpu.SemaphoreType.DMA((32,)), pltpu.SemaphoreType.DMA((32,))],
        compiler_params=pltpu.CompilerParams(
            collective_id=0, has_side_effects=True, vmem_limit_bytes=48 * 1024 * 1024
        ),
        cost_estimate=pl.CostEstimate(
            flops=1_000_000_000, bytes_accessed=4_000_000, transcendentals=600_000
        ),
    )(sequence_acts, jnp.transpose(taps, (2, 0, 1)), dilations, left_link, projection, head_cotangent)
    return grad, weight, jnp.transpose(tap_grads, (1, 2, 0))


def solution(mesh):
    placed = (P("dp", None, "seq"), P(), P(), P("dp", None), P("dp", None), P("dp", "seq", None))
    return jax.shard_map(
        local,
        mesh=mesh,
        in_specs=placed,
        out_specs=(P("dp", None, "seq"), P("seq", None), P()),
        check_vma=False,
    )
```

```python
import functools
import math

import jax
import jax.numpy as jnp
from jax import lax
from jax.experimental import pallas as pl
from jax.experimental.pallas import tpu as pltpu
from jax.sharding import PartitionSpec as P

MESH = pl.DeviceIdType.MESH
BF = jnp.bfloat16
F32 = jnp.float32

C = 768
ROWS = 256
HALF = 128
SEQ = 64
DP = 8
OWN = 14
PAD = 16
SLAB = 64
LAST_DILATION = 8
Z_PART, X_PART, SIB_PART = 32, 36, 40
FAR_FIRST = sorted(
    range(1, SEQ),
    key=lambda m: -((0, 1, 2, 2)[m >> 4] + (0, 1, 2, 2, 4, 3, 2, 2)[(m >> 1) & 7]),
)
GELU = 0.7978845608028654


def gelu_pair(v):
    th = jnp.tanh(GELU * (v + 0.044715 * v * v * v))
    act = 0.5 * v * (1.0 + th)
    slope = 0.5 * (1.0 + th) + 0.5 * v * (1.0 - th * th) * GELU * (1.0 + 3.0 * 0.044715 * v * v)
    return act, slope


def rounded(v):
    return v.astype(BF).astype(F32)


def earlier(tiles, lane, d):
    turned = [pltpu.roll(t, d, 1) for t in tiles]
    return [jnp.where(lane < d, turned[j - 1], turned[j]) for j in range(len(tiles))]


def later(tiles, lane, d):
    turned = [pltpu.roll(t, HALF - d, 1) for t in tiles]
    n = len(tiles)
    return [jnp.where(lane >= HALF - d, turned[(j + 1) % n], turned[j]) for j in range(n)]


def kernel(
    x_in, taps_in, dil_in, link_in, proj_in, cot_in,
    out_ref, pg_ref, tg_ref,
    x_ref, taps_ref, proj_ref, cot_ref, dil_ref, link_ref,
    stage, cot, cot_sib, pfull, edge_s, edge_r, cot_t, halo, wide,
    a0, a1, s0, s1, x2, pooled, pooled_sib, g2, g1, moved, prods,
    a_s1, a_r1, a_s2, a_r2, a_s3, a_r3, a_r4, b_s1, b_r1, b_s2, b_r2, b_r3,
    t_s, t_r1, t_r2, t_r3, t_f,
    send, recv, load,
):
    s = lax.axis_index("seq")
    d = lax.axis_index("dp")
    core = s % 2
    y = (s // 2) % 8
    zl = s // 16
    x = d % 4
    zh = d // 4
    z8 = zh * 4 + zl
    sib = s + 1 - 2 * core

    def at_x(k):
        return {"seq": s, "dp": zh * 4 + (x + k) % 4}

    def at_x_core(xx, cc):
        return {"seq": s - core + cc, "dp": zh * 4 + xx}

    def at_y(yy):
        return {"seq": zl * 16 + yy * 2 + core, "dp": d}

    def at_z(zz):
        return {"seq": (zz % 4) * 16 + y * 2 + core, "dp": (zz // 4) * 4 + x}

    whole = {
        0: edge_s.at[0], 1: edge_s.at[0], 6: stage.at[pl.ds(0, SEQ - 1)], 7: pooled, 12: cot_sib,
        13: b_r1.at[pl.ds(0, 7)], 14: a_r1.at[pl.ds(0, 3)], 21: cot_t.at[pl.ds(0, PAD)], 22: cot_t.at[pl.ds(0, PAD)],
        23: t_r1.at[pl.ds(0, 7)], 24: b_r2.at[pl.ds(0, 7)], 25: a_r2.at[pl.ds(0, 7)],
        26: t_r2.at[pl.ds(0, 7)], 27: b_r3.at[pl.ds(0, 3)], 28: a_r3.at[pl.ds(0, 7)],
        29: t_r3.at[pl.ds(0, 7)], 30: a_r4.at[pl.ds(0, 3)], 31: t_f.at[0],
        3: pfull.at[0, pl.ds(0, 3)], 4: pfull.at[0, pl.ds(0, 4)],
    }
    for i in range(4):
        whole[Z_PART + i] = pfull.at[0, 0, pl.ds(0, PAD)]
        whole[X_PART + i] = pfull.at[0, pl.ds(0, 3), pl.ds(0, PAD)]
        whole[SIB_PART + i] = pfull.at[0, pl.ds(0, 4), pl.ds(0, PAD)]
    started, ended = [], []
    sibling = {"seq": sib, "dp": d}

    def push(src, dst, i, where):
        if i not in started:
            started.append(i)
        pltpu.make_async_remote_copy(
            src_ref=src, dst_ref=dst, send_sem=send.at[i], recv_sem=recv.at[i],
            device_id=where, device_id_type=MESH,
        ).start()

    def dummy(i):
        ref = whole[i]
        return pltpu.make_async_remote_copy(
            src_ref=ref, dst_ref=ref, send_sem=send.at[i], recv_sem=recv.at[i],
            device_id={"seq": sib, "dp": d}, device_id_type=MESH,
        )

    def arrived(i):
        ended.append(i)
        dummy(i).wait_recv()

    def finish():
        for i in started:
            if i not in ended:
                arrived(i)
            if i in range(Z_PART, Z_PART + 4):
                @pl.when((zl == 0) | (zl == 3))
                def _():
                    dummy(i).wait_send()
                    dummy(i).wait_send()
            else:
                dummy(i).wait_send()

    loads = [
        pltpu.make_async_copy(a, b, load.at[i])
        for i, (a, b) in enumerate(
            (
                (cot_in, cot_ref), (x_in, x_ref), (proj_in, proj_ref), (taps_in, taps_ref),
                (dil_in, dil_ref), (link_in, link_ref),
            )
        )
    ]
    for copy in loads:
        copy.start()

    barrier = pltpu.get_barrier_semaphore()

    def greet(where):
        pl.semaphore_signal(barrier, inc=1, device_id=where, device_id_type=MESH)

    @pl.loop(1, SEQ)
    def _(k):
        greet({"seq": (s + k) % SEQ, "dp": d})

    for k in range(4):
        greet({"seq": ((zl + k) % 4) * 16 + y * 2 + core, "dp": (1 - zh) * 4 + x})
    for k in range(1, 4):
        greet(at_x(k))
        greet({"seq": sib, "dp": zh * 4 + (x + k) % 4})

    lane = lax.broadcasted_iota(jnp.int32, (1, HALF), 1)

    def pack_edges(read, dst):
        for side in range(2):
            total = None
            for k in range(8):
                rows = pl.ds(96 * k, 96)
                part = read(1 - side, rows).astype(F32)
                part = pltpu.roll(part, (16 * k + 16 * (1 - side)) % HALF, 1)
                keep = (lane >= 16 * k) & (lane < 16 * k + 16)
                total = jnp.where(keep, part, 0.0 if total is None else total)
            dst[side] = total.astype(BF)

    def halo_keep(width):
        return ((lane < width) & right_linked) | ((lane >= HALF - width) & left_linked)

    def unpack_edges(src, dst):
        from_left = src[0].astype(F32)
        from_right = src[1].astype(F32)
        for k in range(8):
            left = pltpu.roll(from_left, (HALF - 16 - 16 * k) % HALF, 1)
            right = pltpu.roll(from_right, (HALF - 16 * k) % HALF, 1)
            tile = jnp.where(lane < HALF // 2, right, left)
            dst[pl.ds(96 * k, 96), :] = jnp.where(halo_keep(16), tile, 0.0)

    loads[0].wait()
    for t in range(SEQ):
        block = cot_ref[0, :, pl.ds(HALF * t, HALF)]
        stage[t] = jnp.concatenate(
            [block.astype(F32), jnp.zeros((PAD - OWN, HALF), F32)], axis=0
        ).astype(BF)

    loads[1].wait()
    pack_edges(lambda j, rows: x_ref[0, rows, pl.ds(HALF * j, HALF)], edge_s)

    loads[2].wait()
    row = lax.broadcasted_iota(jnp.int32, (64, 112), 0)
    col = lax.broadcasted_iota(jnp.int32, (64, 112), 1)
    inner = row % PAD
    source = OWN * (2 * (row // PAD) + core) + inner
    pick = jnp.where((inner < OWN) & (source == col), 1.0, 0.0).astype(BF)
    pfull[core, d] = jnp.dot(pick, proj_ref[...], preferred_element_type=F32).astype(BF)

    pl.semaphore_wait(barrier, SEQ - 1 + 4 + 6)

    push(edge_s.at[0], edge_r.at[0], 0, {"seq": (s + 1) % SEQ, "dp": d})
    push(edge_s.at[1], edge_r.at[1], 1, {"seq": (s + SEQ - 1) % SEQ, "dp": d})
    for edge, step in ((0, -1), (3, 1)):
        @pl.when(zl == edge)
        def _():
            for i in range(4):
                rows = pfull.at[core, d, pl.ds(PAD * i, PAD)]
                for far in (2, 1):
                    push(rows, rows, Z_PART + i, at_z((z8 + 8 + far * step) % 8))
    for k in (2, 1, 3):
        push(pfull.at[core, d], pfull.at[core, d], 3, at_x(k))
    other = (1 - zh) * 4

    def pass_x(i):
        arrived(Z_PART + i)
        rows = pfull.at[core, other + x, pl.ds(PAD * i, PAD)]
        for k in (2, 1, 3):
            push(rows, rows, X_PART + i, at_x(k))

    def pass_core(i):
        arrived(X_PART + i)
        rows = pfull.at[core, pl.ds(other, 4), pl.ds(PAD * i, PAD)]
        push(rows, rows, SIB_PART + i, sibling)

    me = core * 32 + zl * 8 + y
    for m in FAR_FIRST:
        t = s ^ m
        push(stage.at[t], cot.at[me], 6, {"seq": t, "dp": d})

    cot[me] = stage[s]

    for copy in loads[3:]:
        copy.wait()
    left_linked = link_ref[0, s] >= 0
    right_linked = link_ref[0, (s + 1) % SEQ] >= 0
    six = jnp.concatenate([taps_ref[k] for k in range(3)] + [jnp.zeros((2, C), F32)], axis=0)
    six = jnp.transpose(six)
    for i in range(6):
        wide[i] = jnp.broadcast_to(six[:, i:i + 1], (C, HALF))
    d0 = dil_ref[0]

    def weights(rows):
        return [[wide[2 * k + b, rows, :] for k in range(3)] for b in range(2)]

    @pl.loop(0, C // SLAB)
    def _(i):
        rows = pl.ds(pl.multiple_of(i * SLAB, SLAB), SLAB)
        for j in range(2):
            act, slope = gelu_pair(x_ref[0, rows, HALF * j:HALF * (j + 1)].astype(F32))
            a0[j, rows, :] = act
            s0[j, rows, :] = slope

    arrived(0)
    arrived(1)
    unpack_edges(edge_r, halo)

    def forward(first, last):
        @pl.loop(first, last)
        def _(i):
            rows = pl.ds(pl.multiple_of(i * SLAB, SLAB), SLAB)
            w = weights(rows)
            xs = [x_ref[0, rows, :HALF].astype(F32), x_ref[0, rows, HALF:].astype(F32), halo[rows, :]]
            acts = [a0[0, rows, :], a0[1, rows, :], gelu_pair(xs[2])[0]]
            lo, hi = earlier(acts, lane, d0), later(acts, lane, d0)
            ones = []
            acts1 = []
            for j in range(3):
                v = rounded(xs[j] + ((w[0][0] * lo[j] + w[0][1] * acts[j]) + w[0][2] * hi[j]))
                if j == 2:
                    v = jnp.where(halo_keep(8), v, 0.0)
                ones.append(v)
                act, slope = gelu_pair(v)
                acts1.append(act)
                if j < 2:
                    a1[j, rows, :] = act
                s1[j, rows, :] = slope
            lo, hi = earlier(acts1, lane, LAST_DILATION), later(acts1, lane, LAST_DILATION)
            for j in range(2):
                v = ones[j] + ((w[1][0] * lo[j] + w[1][1] * acts1[j]) + w[1][2] * hi[j])
                x2[rows, HALF * j:HALF * (j + 1)] = v.astype(BF)

    forward(0, 4)
    pass_x(0)
    forward(4, 8)
    pass_x(1)
    pass_x(2)
    forward(8, 12)
    pass_x(3)
    arrived(3)
    rows = pfull.at[core, pl.ds(zh * 4, 4)]
    push(rows, rows, 4, sibling)

    two = lax.broadcasted_iota(jnp.int32, (ROWS, HALF), 0) // 2
    pair = two == lax.broadcasted_iota(jnp.int32, (ROWS, HALF), 1)
    halves = jnp.where(pair, 0.5, 0.0).astype(BF)
    pooled[...] = jnp.dot(x2[...], halves, preferred_element_type=F32).astype(BF)
    push(pooled, pooled_sib, 7, {"seq": sib, "dp": d})

    arrived(6)
    push(cot.at[pl.ds((1 - core) * 32, 32)], cot_sib, 12, sibling)
    eye = lax.broadcasted_iota(jnp.int32, (HALF, HALF), 0) == lax.broadcasted_iota(jnp.int32, (HALF, HALF), 1)
    nt = (((1,), (1,)), ((), ()))
    cot_t[:HALF] = lax.dot_general(
        jnp.where(eye, 1.0, 0.0).astype(BF), cot[...].reshape(SEQ * PAD, HALF), nt,
        preferred_element_type=F32,
    ).astype(BF)
    push(cot_t.at[pl.ds(HALF - PAD, PAD)], cot_t.at[pl.ds(HALF + PAD, PAD)], 21, {"seq": (s + 1) % SEQ, "dp": d})
    push(cot_t.at[pl.ds(0, PAD)], cot_t.at[pl.ds(HALF, PAD)], 22, {"seq": (s + SEQ - 1) % SEQ, "dp": d})
    pass_core(0)
    pass_core(1)
    arrived(7)
    arrived(12)
    mine = cot[pl.ds(core * 32, 32)].reshape(512, HALF)
    theirs = cot_sib[...].reshape(512, HALF)
    for j in (2, 0, 1):
        cols = pl.ds(256 * j, 256)
        part = lax.dot_general(mine, pooled[cols, :], nt, preferred_element_type=F32)
        part = part + lax.dot_general(theirs, pooled_sib[cols, :], nt, preferred_element_type=F32)
        part = part.astype(BF)
        if j == 2:
            b_s1[...] = part.reshape(4, 8, PAD, 256)
            @pl.loop(1, 8)
            def _(k):
                yy = (y + k) % 8
                push(b_s1.at[:, yy], b_r1.at[y], 13, at_y(yy))
        else:
            a_s1[2 * j] = part[:, :HALF].reshape(4, 8, PAD, HALF)
            a_s1[2 * j + 1] = part[:, HALF:].reshape(4, 8, PAD, HALF)
    for k in (1, 3, 2):
        push(a_s1.at[(x + k) % 4], a_r1.at[x], 14, at_x(k))
    b_r1[y] = b_s1[:, y]
    a_r1[x] = a_s1[x]

    pass_core(2)
    pass_core(3)
    for i in (4, SIB_PART, SIB_PART + 1, SIB_PART + 2, SIB_PART + 3, 21, 22):
        arrived(i)
    back = jnp.dot(cot_t[...], pfull[...].reshape(SEQ * PAD, C), preferred_element_type=F32)
    back = (0.5 * back).astype(BF)
    ring = 3 * HALF
    shape = (HALF + 2 * PAD, ring)
    at = lax.broadcasted_iota(jnp.int32, shape, 0)
    to = lax.broadcasted_iota(jnp.int32, shape, 1)
    right = (to >= ROWS) & (to < ROWS + 16) & right_linked
    left = (to >= ring - 16) & left_linked
    origin = jnp.where(
        to < ROWS, to // 2,
        jnp.where(right, HALF + (to - ROWS) // 2, jnp.where(left, HALF + 24 + (to - ring + 16) // 2, -1)),
    )
    spread = jnp.where(at == origin, 1.0, 0.0).astype(BF)
    g2[...] = lax.dot_general(
        back, spread, (((0,), (0,)), ((), ())), preferred_element_type=F32
    ).astype(BF)

    def shifts(dist, length):
        at = lax.broadcasted_iota(jnp.int32, (ring, 2 * length), 0)
        to = lax.broadcasted_iota(jnp.int32, (ring, 2 * length), 1)
        low = to < length
        to = jnp.where(low, to - dist + ring, to - length + dist)
        to = jnp.where(to >= ring, to - ring, to)
        return jnp.where(at == to, 1.0, 0.0).astype(BF)

    def keep_product(rows, column, total):
        high = total.astype(BF)
        prods[rows, HALF * column:HALF * (column + 1)] = high
        low = (total - high.astype(F32)).astype(BF)
        prods[rows, HALF * (column + 6):HALF * (column + 7)] = low

    matrix1 = shifts(LAST_DILATION, ring)
    matrix0 = shifts(d0, ROWS)
    moved[...] = jnp.dot(g2[...], matrix1, preferred_element_type=F32)

    @pl.loop(0, C // SLAB)
    def _(i):
        rows = pl.ds(pl.multiple_of(i * SLAB, SLAB), SLAB)
        w = weights(rows)[1]
        g = [g2[rows, HALF * j:HALF * (j + 1)].astype(F32) for j in range(3)]
        lo = [moved[rows, HALF * j:HALF * (j + 1)] for j in range(3)]
        hi = [moved[rows, ring + HALF * j:ring + HALF * (j + 1)] for j in range(3)]
        for j in range(3):
            conv = (w[0] * hi[j] + w[1] * g[j]) + w[2] * lo[j]
            v = g[j] + conv * s1[j, rows, :]
            if j == 2:
                v = jnp.where(halo_keep(8), v, 0.0)
            g1[rows, HALF * j:HALF * (j + 1)] = v.astype(BF)
        for k, part in enumerate((hi, g, lo)):
            keep_product(rows, 2 * k + 1, a1[0, rows, :] * part[0] + a1[1, rows, :] * part[1])

    moved[:, :2 * ROWS] = jnp.dot(g1[...], matrix0, preferred_element_type=F32)

    @pl.loop(0, C // SLAB)
    def _(i):
        rows = pl.ds(pl.multiple_of(i * SLAB, SLAB), SLAB)
        w = weights(rows)[0]
        g = [g1[rows, HALF * j:HALF * (j + 1)].astype(F32) for j in range(2)]
        lo = [moved[rows, HALF * j:HALF * (j + 1)] for j in range(2)]
        hi = [moved[rows, ROWS + HALF * j:ROWS + HALF * (j + 1)] for j in range(2)]
        for j in range(2):
            conv = (w[0] * hi[j] + w[1] * g[j]) + w[2] * lo[j]
            out_ref[0, rows, HALF * j:HALF * (j + 1)] = (g[j] + conv * s0[j, rows, :]).astype(BF)
        for k, part in enumerate((hi, g, lo)):
            keep_product(rows, 2 * k, a0[0, rows, :] * part[0] + a0[1, rows, :] * part[1])

    which = lax.broadcasted_iota(jnp.int32, (8, 12 * HALF), 1) // HALF
    row = lax.broadcasted_iota(jnp.int32, (8, 12 * HALF), 0)
    ones = jnp.where(which % 6 == row, 1.0, 0.0).astype(BF)
    flat = lax.dot_general(ones, prods[...], nt, preferred_element_type=F32)
    t_s[0] = flat[:, :384]
    t_s[1] = flat[:, 384:]
    slot = x * 2 + core
    t_r1[slot] = t_s[core]
    for k in range(4):
        for c in range(2):
            cc = (core + c) % 2
            if k or c:
                push(t_s.at[cc], t_r1.at[slot], 23, at_x_core((x + k) % 4, cc))

    def total(ref):
        parts = [ref[i].astype(F32) for i in range(ref.shape[0])]
        while len(parts) > 1:
            parts = [a + b for a, b in zip(parts[::2], parts[1::2])]
        return parts[0]

    arrived(13)
    b_s2[...] = total(b_r1).astype(BF)
    @pl.loop(1, 8)
    def _(k):
        zz = (z8 + k) % 8
        push(b_s2.at[zz % 4], b_r2.at[z8], 24, at_z(zz))
    b_r2[z8] = b_s2[zl]

    arrived(14)
    a_s2[...] = total(a_r1).astype(BF)
    @pl.loop(1, 8)
    def _(k):
        yy = (y + k) % 8
        push(a_s2.at[:, yy], a_r2.at[y], 25, at_y(yy))
    a_r2[y] = a_s2[:, y]

    arrived(23)
    t_r2[y] = total(t_r1)
    @pl.loop(1, 8)
    def _(k):
        push(t_r2.at[y], t_r2.at[y], 26, at_y((y + k) % 8))

    arrived(24)
    b_r3[x] = total(b_r2)
    for k in (1, 3, 2):
        push(b_r3.at[x], b_r3.at[x], 27, at_x(k))

    arrived(25)
    a_s3[...] = total(a_r2).astype(BF)
    @pl.loop(1, 8)
    def _(k):
        zz = (z8 + k) % 8
        push(a_s3.at[zz % 4], a_r3.at[z8], 28, at_z(zz))
    a_r3[z8] = a_s3[zl]

    arrived(26)
    t_r3[z8] = total(t_r2)
    @pl.loop(1, 8)
    def _(k):
        push(t_r3.at[z8], t_r3.at[z8], 29, at_z((z8 + k) % 8))

    arrived(28)
    a_r4[x] = total(a_r3)
    for k in (1, 3, 2):
        push(a_r4.at[x], a_r4.at[x], 30, at_x(k))

    arrived(29)
    t_f[core] = total(t_r3)
    push(t_f.at[core], t_f.at[core], 31, sibling)

    scale = 1.0 / math.sqrt(SEQ * DP * HALF)
    arrived(27)
    pg_ref[:, 512:] = total(b_r3)[:OWN] * scale
    arrived(30)
    for j in range(4):
        pg_ref[:, HALF * j:HALF * (j + 1)] = a_r4[j][:OWN] * scale
    arrived(31)
    for h in range(2):
        for k in range(3):
            tg_ref[k, :, 384 * h:384 * (h + 1)] = t_f[h][2 * k:2 * k + 2] * scale

    finish()


SCRATCH = [
    ((1, C, ROWS), BF),
    ((3, 2, C), F32),
    ((112, C), BF),
    ((1, OWN, SEQ * HALF), BF),
    ((SEQ, PAD, HALF), BF),
    ((SEQ, PAD, HALF), BF),
    ((32, PAD, HALF), BF),
    ((2, DP, 64, C), BF),
    ((2, 96, HALF), BF),
    ((2, 96, HALF), BF),
    ((HALF + 2 * PAD, SEQ * PAD), BF),
    ((C, HALF), F32),
    ((6, C, HALF), F32),
    ((2, C, HALF), F32),
    ((2, C, HALF), F32),
    ((2, C, HALF), F32),
    ((3, C, HALF), F32),
    ((C, ROWS), BF),
    ((C, HALF), BF),
    ((C, HALF), BF),
    ((C, 3 * HALF), BF),
    ((C, 3 * HALF), BF),
    ((C, 6 * HALF), F32),
    ((C, 12 * HALF), BF),
    ((4, 4, 8, PAD, HALF), BF),
    ((4, 4, 8, PAD, HALF), BF),
    ((4, 8, PAD, HALF), BF),
    ((8, 4, PAD, HALF), BF),
    ((4, PAD, HALF), BF),
    ((8, PAD, HALF), BF),
    ((4, PAD, HALF), F32),
    ((4, 8, PAD, 256), BF),
    ((8, 4, PAD, 256), BF),
    ((4, PAD, 256), BF),
    ((8, PAD, 256), BF),
    ((4, PAD, 256), F32),
    ((2, 8, 384), F32),
    ((8, 8, 384), F32),
    ((8, 8, 384), F32),
    ((8, 8, 384), F32),
    ((2, 8, 384), F32),
]


def local(sequence_acts, taps, dilations, left_link, projection, head_cotangent):
    vmem = pl.BlockSpec(memory_space=pltpu.VMEM)
    hbm = pl.BlockSpec(memory_space=pltpu.HBM)
    grad, weight, tap_grads = pl.pallas_call(
        kernel,
        out_shape=(
            jax.ShapeDtypeStruct((1, C, ROWS), BF),
            jax.ShapeDtypeStruct((OWN, C), F32),
            jax.ShapeDtypeStruct((3, 2, C), F32),
        ),
        in_specs=[hbm] * 6,
        out_specs=(vmem, vmem, vmem),
        scratch_shapes=[pltpu.VMEM(shape, kind) for shape, kind in SCRATCH[:4]]
        + [pltpu.SMEM((2,), jnp.int32), pltpu.SMEM((1, SEQ), jnp.int32)]
        + [pltpu.VMEM(shape, kind) for shape, kind in SCRATCH[4:]]
        + [pltpu.SemaphoreType.DMA((44,)), pltpu.SemaphoreType.DMA((44,)), pltpu.SemaphoreType.DMA((6,))],
        compiler_params=pltpu.CompilerParams(
            collective_id=0, has_side_effects=True, vmem_limit_bytes=60 * 1024 * 1024
        ),
        cost_estimate=pl.CostEstimate(
            flops=1_000_000_000, bytes_accessed=4_000_000, transcendentals=600_000
        ),
    )(sequence_acts, jnp.transpose(taps, (2, 0, 1)), dilations, left_link, projection, head_cotangent)
    return grad, weight, jnp.transpose(tap_grads, (1, 2, 0))


def solution(mesh):
    placed = (P("dp", None, "seq"), P(), P(), P("dp", None), P("dp", None), P("dp", "seq", None))
    return jax.shard_map(
        local,
        mesh=mesh,
        in_specs=placed,
        out_specs=(P("dp", None, "seq"), P("seq", None), P()),
        check_vma=False,
    )
```

```python
import functools
import math

import jax
import jax.numpy as jnp
from jax import lax
from jax.experimental import pallas as pl
from jax.experimental.pallas import tpu as pltpu
from jax.sharding import PartitionSpec as P

MESH = pl.DeviceIdType.MESH
BF = jnp.bfloat16
F32 = jnp.float32

C = 768
ROWS = 256
HALF = 128
SEQ = 64
DP = 8
OWN = 14
PAD = 16
SLAB = 64
LAST_DILATION = 8
Z_PART, X_PART, SIB_PART = 32, 36, 40
FAR_FIRST = sorted(
    range(1, SEQ),
    key=lambda m: -((0, 1, 2, 2)[m >> 4] + (0, 1, 2, 2, 4, 3, 2, 2)[(m >> 1) & 7]),
)
FAR_RING = (4, 3, 5, 2, 6, 1, 7)
GELU = 0.7978845608028654


def gelu_pair(v):
    th = jnp.tanh(GELU * (v + 0.044715 * v * v * v))
    act = 0.5 * v * (1.0 + th)
    slope = 0.5 * (1.0 + th) + 0.5 * v * (1.0 - th * th) * GELU * (1.0 + 3.0 * 0.044715 * v * v)
    return act, slope


def rounded(v):
    return v.astype(BF).astype(F32)


def earlier(tiles, lane, d):
    turned = [pltpu.roll(t, d, 1) for t in tiles]
    return [jnp.where(lane < d, turned[j - 1], turned[j]) for j in range(len(tiles))]


def later(tiles, lane, d):
    turned = [pltpu.roll(t, HALF - d, 1) for t in tiles]
    n = len(tiles)
    return [jnp.where(lane >= HALF - d, turned[(j + 1) % n], turned[j]) for j in range(n)]


def kernel(
    x_in, taps_in, dil_in, link_in, proj_in, cot_in,
    out_hbm, pg_hbm, tg_hbm,
    out_ref, pg_ref, tg_ref,
    x_ref, taps_ref, proj_ref, cot_ref, dil_ref, link_ref,
    stage, cot, cot_sib, pfull, edge_s, edge_r, cot_t, halo, wide,
    a0, a1, s0, s1, x2, pooled, pooled_sib, g2, g1, moved, prods,
    a_s1, a_r1, a_s2, a_r2, a_s3, a_r3, a_r4, b_s1, b_r1, b_s2, b_r2, b_r3,
    t_r1, t_r2, t_r3,
    send, recv, load, store,
):
    s = lax.axis_index("seq")
    d = lax.axis_index("dp")
    core = s % 2
    y = (s // 2) % 8
    zl = s // 16
    x = d % 4
    zh = d // 4
    z8 = zh * 4 + zl
    sib = s + 1 - 2 * core

    def at_x(k):
        return {"seq": s, "dp": zh * 4 + (x + k) % 4}

    def at_x_core(xx, cc):
        return {"seq": s - core + cc, "dp": zh * 4 + xx}

    def at_y(yy):
        return {"seq": zl * 16 + yy * 2 + core, "dp": d}

    def at_z(zz):
        return {"seq": (zz % 4) * 16 + y * 2 + core, "dp": (zz // 4) * 4 + x}

    whole = {
        0: edge_s.at[0], 1: edge_s.at[0], 6: stage.at[pl.ds(0, SEQ - 1)], 7: pooled, 12: cot_sib,
        13: b_r1.at[pl.ds(0, 7)], 14: a_r1.at[pl.ds(0, 3)], 21: cot_t.at[pl.ds(0, PAD)], 22: cot_t.at[pl.ds(0, PAD)],
        23: t_r1.at[pl.ds(0, 7)], 24: b_r2.at[pl.ds(0, 7)], 25: a_r2.at[pl.ds(0, 7)], 28: a_r3.at[pl.ds(0, 7)],
        26: t_r2.at[pl.ds(0, 7)], 27: b_r3.at[pl.ds(0, 3)],
        29: t_r3.at[pl.ds(0, 7)], 30: a_r4.at[pl.ds(0, 3)],
        3: pfull.at[0, pl.ds(0, 3)], 4: pfull.at[0, pl.ds(0, 4)],
    }
    for i in range(4):
        whole[Z_PART + i] = pfull.at[0, 0, pl.ds(0, PAD)]
        whole[X_PART + i] = pfull.at[0, pl.ds(0, 3), pl.ds(0, PAD)]
        whole[SIB_PART + i] = pfull.at[0, pl.ds(0, 4), pl.ds(0, PAD)]
    started, ended = [], []
    sibling = {"seq": sib, "dp": d}

    def push(src, dst, i, where):
        if i not in started:
            started.append(i)
        pltpu.make_async_remote_copy(
            src_ref=src, dst_ref=dst, send_sem=send.at[i], recv_sem=recv.at[i],
            device_id=where, device_id_type=MESH,
        ).start()

    def dummy(i):
        ref = whole[i]
        return pltpu.make_async_remote_copy(
            src_ref=ref, dst_ref=ref, send_sem=send.at[i], recv_sem=recv.at[i],
            device_id={"seq": sib, "dp": d}, device_id_type=MESH,
        )

    def arrived(i):
        ended.append(i)
        dummy(i).wait_recv()

    def finish():
        for i in started:
            if i not in ended:
                arrived(i)
            if i in range(Z_PART, Z_PART + 4):
                @pl.when((zl == 0) | (zl == 3))
                def _():
                    dummy(i).wait_send()
                    dummy(i).wait_send()
            else:
                dummy(i).wait_send()

    loads = [
        pltpu.make_async_copy(a, b, load.at[i])
        for i, (a, b) in enumerate(
            (
                (cot_in, cot_ref), (x_in, x_ref), (proj_in, proj_ref), (taps_in, taps_ref),
                (dil_in, dil_ref), (link_in, link_ref),
            )
        )
    ]
    for copy in loads:
        copy.start()

    barrier = pltpu.get_barrier_semaphore()

    def greet(where):
        pl.semaphore_signal(barrier, inc=1, device_id=where, device_id_type=MESH)

    @pl.loop(1, SEQ)
    def _(k):
        greet({"seq": (s + k) % SEQ, "dp": d})

    for k in range(4):
        greet({"seq": ((zl + k) % 4) * 16 + y * 2 + core, "dp": (1 - zh) * 4 + x})
    for k in range(1, 4):
        greet(at_x(k))
        greet({"seq": sib, "dp": zh * 4 + (x + k) % 4})

    lane = lax.broadcasted_iota(jnp.int32, (1, HALF), 1)

    def pack_edges(read, dst):
        for side in range(2):
            total = None
            for k in range(8):
                rows = pl.ds(96 * k, 96)
                part = read(1 - side, rows).astype(F32)
                part = pltpu.roll(part, (16 * k + 16 * (1 - side)) % HALF, 1)
                keep = (lane >= 16 * k) & (lane < 16 * k + 16)
                total = jnp.where(keep, part, 0.0 if total is None else total)
            dst[side] = total.astype(BF)

    def halo_keep(width):
        return ((lane < width) & right_linked) | ((lane >= HALF - width) & left_linked)

    def unpack_edges(src, dst):
        from_left = src[0].astype(F32)
        from_right = src[1].astype(F32)
        for k in range(8):
            left = pltpu.roll(from_left, (HALF - 16 - 16 * k) % HALF, 1)
            right = pltpu.roll(from_right, (HALF - 16 * k) % HALF, 1)
            tile = jnp.where(lane < HALF // 2, right, left)
            dst[pl.ds(96 * k, 96), :] = jnp.where(halo_keep(16), tile, 0.0)

    loads[0].wait()
    for t in range(SEQ):
        block = cot_ref[0, :, pl.ds(HALF * t, HALF)]
        stage[t] = jnp.concatenate(
            [block.astype(F32), jnp.zeros((PAD - OWN, HALF), F32)], axis=0
        ).astype(BF)

    loads[1].wait()
    pack_edges(lambda j, rows: x_ref[0, rows, pl.ds(HALF * j, HALF)], edge_s)

    loads[2].wait()
    row = lax.broadcasted_iota(jnp.int32, (64, 112), 0)
    col = lax.broadcasted_iota(jnp.int32, (64, 112), 1)
    inner = row % PAD
    source = OWN * (2 * (row // PAD) + core) + inner
    pick = jnp.where((inner < OWN) & (source == col), 1.0, 0.0).astype(BF)
    pfull[core, d] = jnp.dot(pick, proj_ref[...], preferred_element_type=F32).astype(BF)

    pl.semaphore_wait(barrier, SEQ - 1 + 4 + 6)

    push(edge_s.at[0], edge_r.at[0], 0, {"seq": (s + 1) % SEQ, "dp": d})
    push(edge_s.at[1], edge_r.at[1], 1, {"seq": (s + SEQ - 1) % SEQ, "dp": d})
    for edge, step in ((0, -1), (3, 1)):
        @pl.when(zl == edge)
        def _():
            for i in range(4):
                rows = pfull.at[core, d, pl.ds(PAD * i, PAD)]
                for far in (2, 1):
                    push(rows, rows, Z_PART + i, at_z((z8 + 8 + far * step) % 8))
    for k in (2, 1, 3):
        push(pfull.at[core, d], pfull.at[core, d], 3, at_x(k))
    other = (1 - zh) * 4

    def pass_x(i):
        arrived(Z_PART + i)
        rows = pfull.at[core, other + x, pl.ds(PAD * i, PAD)]
        for k in (2, 1, 3):
            push(rows, rows, X_PART + i, at_x(k))

    def pass_core(i):
        arrived(X_PART + i)
        rows = pfull.at[core, pl.ds(other, 4), pl.ds(PAD * i, PAD)]
        push(rows, rows, SIB_PART + i, sibling)

    me = core * 32 + zl * 8 + y
    for m in FAR_FIRST:
        t = s ^ m
        push(stage.at[t], cot.at[me], 6, {"seq": t, "dp": d})

    cot[me] = stage[s]

    for copy in loads[3:]:
        copy.wait()
    left_linked = link_ref[0, s] >= 0
    right_linked = link_ref[0, (s + 1) % SEQ] >= 0
    six = jnp.concatenate([taps_ref[k] for k in range(3)] + [jnp.zeros((2, C), F32)], axis=0)
    six = jnp.transpose(six)
    for i in range(6):
        wide[i] = jnp.broadcast_to(six[:, i:i + 1], (C, HALF))
    d0 = dil_ref[0]

    def weights(rows):
        return [[wide[2 * k + b, rows, :] for k in range(3)] for b in range(2)]

    @pl.loop(0, C // SLAB)
    def _(i):
        rows = pl.ds(pl.multiple_of(i * SLAB, SLAB), SLAB)
        for j in range(2):
            act, slope = gelu_pair(x_ref[0, rows, HALF * j:HALF * (j + 1)].astype(F32))
            a0[j, rows, :] = act
            s0[j, rows, :] = slope

    arrived(0)
    arrived(1)
    unpack_edges(edge_r, halo)

    def forward(first, last):
        @pl.loop(first, last)
        def _(i):
            rows = pl.ds(pl.multiple_of(i * SLAB, SLAB), SLAB)
            w = weights(rows)
            xs = [x_ref[0, rows, :HALF].astype(F32), x_ref[0, rows, HALF:].astype(F32), halo[rows, :]]
            acts = [a0[0, rows, :], a0[1, rows, :], gelu_pair(xs[2])[0]]
            lo, hi = earlier(acts, lane, d0), later(acts, lane, d0)
            ones = []
            acts1 = []
            for j in range(3):
                v = rounded(xs[j] + ((w[0][0] * lo[j] + w[0][1] * acts[j]) + w[0][2] * hi[j]))
                if j == 2:
                    v = jnp.where(halo_keep(8), v, 0.0)
                ones.append(v)
                act, slope = gelu_pair(v)
                acts1.append(act)
                if j < 2:
                    a1[j, rows, :] = act
                s1[j, rows, :] = slope
            lo, hi = earlier(acts1, lane, LAST_DILATION), later(acts1, lane, LAST_DILATION)
            for j in range(2):
                v = ones[j] + ((w[1][0] * lo[j] + w[1][1] * acts1[j]) + w[1][2] * hi[j])
                x2[rows, HALF * j:HALF * (j + 1)] = v.astype(BF)

    forward(0, 4)
    pass_x(0)
    forward(4, 8)
    pass_x(1)
    pass_x(2)
    forward(8, 12)
    pass_x(3)
    arrived(3)
    rows = pfull.at[core, pl.ds(zh * 4, 4)]
    push(rows, rows, 4, sibling)

    two = lax.broadcasted_iota(jnp.int32, (ROWS, HALF), 0) // 2
    pair = two == lax.broadcasted_iota(jnp.int32, (ROWS, HALF), 1)
    halves = jnp.where(pair, 0.5, 0.0).astype(BF)
    pooled[...] = jnp.dot(x2[...], halves, preferred_element_type=F32).astype(BF)
    push(pooled, pooled_sib, 7, {"seq": sib, "dp": d})

    arrived(6)
    push(cot.at[pl.ds((1 - core) * 32, 32)], cot_sib, 12, sibling)
    eye = lax.broadcasted_iota(jnp.int32, (HALF, HALF), 0) == lax.broadcasted_iota(jnp.int32, (HALF, HALF), 1)
    nt = (((1,), (1,)), ((), ()))
    cot_t[:HALF] = lax.dot_general(
        jnp.where(eye, 1.0, 0.0).astype(BF), cot[...].reshape(SEQ * PAD, HALF), nt,
        preferred_element_type=F32,
    ).astype(BF)
    push(cot_t.at[pl.ds(HALF - PAD, PAD)], cot_t.at[pl.ds(HALF + PAD, PAD)], 21, {"seq": (s + 1) % SEQ, "dp": d})
    push(cot_t.at[pl.ds(0, PAD)], cot_t.at[pl.ds(HALF, PAD)], 22, {"seq": (s + SEQ - 1) % SEQ, "dp": d})
    arrived(7)
    arrived(12)
    mine = cot[pl.ds(core * 32, 32)].reshape(512, HALF)
    theirs = cot_sib[...].reshape(512, HALF)
    for j in (2, 0, 1):
        cols = pl.ds(256 * j, 256)
        part = lax.dot_general(mine, pooled[cols, :], nt, preferred_element_type=F32)
        part = part + lax.dot_general(theirs, pooled_sib[cols, :], nt, preferred_element_type=F32)
        part = part.astype(BF)
        if j == 2:
            b_s1[...] = part.reshape(4, 8, PAD, 256)
            @pl.loop(1, 8)
            def _(k):
                yy = (y + k) % 8
                push(b_s1.at[:, yy], b_r1.at[y], 13, at_y(yy))
        else:
            a_s1[2 * j] = part[:, :HALF].reshape(4, 8, PAD, HALF)
            a_s1[2 * j + 1] = part[:, HALF:].reshape(4, 8, PAD, HALF)
    for k in (1, 3, 2):
        push(a_s1.at[(x + k) % 4], a_r1.at[x], 14, at_x(k))
    b_r1[y] = b_s1[:, y]
    a_r1[x] = a_s1[x]

    for i in range(4):
        pass_core(i)
    for i in (4, SIB_PART, SIB_PART + 1, SIB_PART + 2, SIB_PART + 3, 21, 22):
        arrived(i)
    back = jnp.dot(cot_t[...], pfull[...].reshape(SEQ * PAD, C), preferred_element_type=F32)
    back = (0.5 * back).astype(BF)
    ring = 3 * HALF
    shape = (HALF + 2 * PAD, ring)
    at = lax.broadcasted_iota(jnp.int32, shape, 0)
    to = lax.broadcasted_iota(jnp.int32, shape, 1)
    right = (to >= ROWS) & (to < ROWS + 16) & right_linked
    left = (to >= ring - 16) & left_linked
    origin = jnp.where(
        to < ROWS, to // 2,
        jnp.where(right, HALF + (to - ROWS) // 2, jnp.where(left, HALF + 24 + (to - ring + 16) // 2, -1)),
    )
    spread = jnp.where(at == origin, 1.0, 0.0).astype(BF)
    g2[...] = lax.dot_general(
        back, spread, (((0,), (0,)), ((), ())), preferred_element_type=F32
    ).astype(BF)

    def shifts(dist, length):
        at = lax.broadcasted_iota(jnp.int32, (ring, 2 * length), 0)
        to = lax.broadcasted_iota(jnp.int32, (ring, 2 * length), 1)
        low = to < length
        to = jnp.where(low, to - dist + ring, to - length + dist)
        to = jnp.where(to >= ring, to - ring, to)
        return jnp.where(at == to, 1.0, 0.0).astype(BF)

    def keep_product(rows, column, total):
        high = total.astype(BF)
        prods[rows, HALF * column:HALF * (column + 1)] = high
        low = (total - high.astype(F32)).astype(BF)
        prods[rows, HALF * (column + 6):HALF * (column + 7)] = low

    matrix1 = shifts(LAST_DILATION, ring)
    matrix0 = shifts(d0, ROWS)
    moved[...] = jnp.dot(g2[...], matrix1, preferred_element_type=F32)

    @pl.loop(0, C // SLAB)
    def _(i):
        rows = pl.ds(pl.multiple_of(i * SLAB, SLAB), SLAB)
        w = weights(rows)[1]
        g = [g2[rows, HALF * j:HALF * (j + 1)].astype(F32) for j in range(3)]
        lo = [moved[rows, HALF * j:HALF * (j + 1)] for j in range(3)]
        hi = [moved[rows, ring + HALF * j:ring + HALF * (j + 1)] for j in range(3)]
        for j in range(3):
            conv = (w[0] * hi[j] + w[1] * g[j]) + w[2] * lo[j]
            v = g[j] + conv * s1[j, rows, :]
            if j == 2:
                v = jnp.where(halo_keep(8), v, 0.0)
            g1[rows, HALF * j:HALF * (j + 1)] = v.astype(BF)
        for k, part in enumerate((hi, g, lo)):
            keep_product(rows, 2 * k + 1, a1[0, rows, :] * part[0] + a1[1, rows, :] * part[1])

    moved[:, :2 * ROWS] = jnp.dot(g1[...], matrix0, preferred_element_type=F32)

    @pl.loop(0, C // SLAB)
    def _(i):
        rows = pl.ds(pl.multiple_of(i * SLAB, SLAB), SLAB)
        w = weights(rows)[0]
        g = [g1[rows, HALF * j:HALF * (j + 1)].astype(F32) for j in range(2)]
        lo = [moved[rows, HALF * j:HALF * (j + 1)] for j in range(2)]
        hi = [moved[rows, ROWS + HALF * j:ROWS + HALF * (j + 1)] for j in range(2)]
        for j in range(2):
            conv = (w[0] * hi[j] + w[1] * g[j]) + w[2] * lo[j]
            out_ref[0, rows, HALF * j:HALF * (j + 1)] = (g[j] + conv * s0[j, rows, :]).astype(BF)
        for k, part in enumerate((hi, g, lo)):
            keep_product(rows, 2 * k, a0[0, rows, :] * part[0] + a0[1, rows, :] * part[1])

    stores = [
        pltpu.make_async_copy(a, b, store.at[i])
        for i, (a, b) in enumerate(((out_ref, out_hbm), (pg_ref, pg_hbm), (tg_ref, tg_hbm)))
    ]
    stores[0].start()
    which = lax.broadcasted_iota(jnp.int32, (8, 12 * HALF), 1) // HALF
    row = lax.broadcasted_iota(jnp.int32, (8, 12 * HALF), 0)
    ones = jnp.where(which % 6 == row, 1.0, 0.0).astype(BF)
    flat = lax.dot_general(ones, prods[...], nt, preferred_element_type=F32)
    slot = x * 2 + core
    t_r1[slot] = jnp.concatenate([flat[:, :384], flat[:, 384:]], axis=0).astype(BF)
    for k in (2, 1, 3, 0):
        for cc in range(2):
            if k:
                push(t_r1.at[slot], t_r1.at[slot], 23, at_x_core((x + k) % 4, cc))
    push(t_r1.at[slot], t_r1.at[slot], 23, sibling)

    def total(ref):
        parts = [ref[i].astype(F32) for i in range(ref.shape[0])]
        while len(parts) > 1:
            parts = [a + b for a, b in zip(parts[::2], parts[1::2])]
        return parts[0]

    arrived(13)
    b_s2[...] = total(b_r1).astype(BF)
    for k in FAR_RING:
        zz = (z8 + k) % 8
        push(b_s2.at[zz % 4], b_r2.at[z8], 24, at_z(zz))
    b_r2[z8] = b_s2[zl]

    arrived(14)
    a_s2[...] = total(a_r1).astype(BF)
    for k in FAR_RING:
        yy = (y + k) % 8
        push(a_s2.at[:, yy], a_r2.at[y], 25, at_y(yy))
    a_r2[y] = a_s2[:, y]

    arrived(23)
    t_r2[z8] = total(t_r1).astype(BF)
    for k in FAR_RING:
        push(t_r2.at[z8], t_r2.at[z8], 26, at_z((z8 + k) % 8))

    arrived(24)
    b_r3[x] = total(b_r2)
    for k in (1, 3, 2):
        push(b_r3.at[x], b_r3.at[x], 27, at_x(k))

    arrived(25)
    a_s3[...] = total(a_r2).astype(BF)
    for k in FAR_RING:
        zz = (z8 + k) % 8
        push(a_s3.at[zz % 4], a_r3.at[z8], 28, at_z(zz))
    a_r3[z8] = a_s3[zl]

    arrived(26)
    t_r3[y] = total(t_r2).astype(BF)
    for k in FAR_RING:
        push(t_r3.at[y], t_r3.at[y], 29, at_y((y + k) % 8))

    arrived(28)
    a_r4[x] = total(a_r3)
    for k in (2, 1, 3):
        push(a_r4.at[x], a_r4.at[x], 30, at_x(k))

    arrived(29)
    taps_total = total(t_r3)

    scale = 1.0 / math.sqrt(SEQ * DP * HALF)
    arrived(27)
    pg_ref[:, 512:] = total(b_r3)[:OWN] * scale
    arrived(30)
    for j in range(4):
        pg_ref[:, HALF * j:HALF * (j + 1)] = a_r4[j][:OWN] * scale
    for h in range(2):
        for k in range(3):
            tg_ref[k, :, 384 * h:384 * (h + 1)] = taps_total[8 * h + 2 * k:8 * h + 2 * k + 2] * scale

    stores[1].start()
    stores[2].start()
    finish()
    for copy in stores:
        copy.wait()


def hand_over(*refs):
    held, sems = refs[6:9], refs[9]
    loads = [pltpu.make_async_copy(refs[i], held[i], sems.at[i]) for i in range(3)]
    stores = [pltpu.make_async_copy(held[i], refs[3 + i], sems.at[3 + i]) for i in range(3)]
    for copy in loads:
        copy.start()
    for load, store in zip(loads, stores):
        load.wait()
        store.start()
    for copy in stores:
        copy.wait()


SCRATCH = [
    ((1, C, ROWS), BF),
    ((OWN, C), F32),
    ((3, 2, C), F32),
    ((1, C, ROWS), BF),
    ((3, 2, C), F32),
    ((112, C), BF),
    ((1, OWN, SEQ * HALF), BF),
    ((SEQ, PAD, HALF), BF),
    ((SEQ, PAD, HALF), BF),
    ((32, PAD, HALF), BF),
    ((2, DP, 64, C), BF),
    ((2, 96, HALF), BF),
    ((2, 96, HALF), BF),
    ((HALF + 2 * PAD, SEQ * PAD), BF),
    ((C, HALF), F32),
    ((6, C, HALF), F32),
    ((2, C, HALF), F32),
    ((2, C, HALF), F32),
    ((2, C, HALF), F32),
    ((3, C, HALF), F32),
    ((C, ROWS), BF),
    ((C, HALF), BF),
    ((C, HALF), BF),
    ((C, 3 * HALF), BF),
    ((C, 3 * HALF), BF),
    ((C, 6 * HALF), F32),
    ((C, 12 * HALF), BF),
    ((4, 4, 8, PAD, HALF), BF),
    ((4, 4, 8, PAD, HALF), BF),
    ((4, 8, PAD, HALF), BF),
    ((8, 4, PAD, HALF), BF),
    ((4, PAD, HALF), BF),
    ((8, PAD, HALF), BF),
    ((4, PAD, HALF), F32),
    ((4, 8, PAD, 256), BF),
    ((8, 4, PAD, 256), BF),
    ((4, PAD, 256), BF),
    ((8, PAD, 256), BF),
    ((4, PAD, 256), F32),
    ((8, PAD, 384), BF),
    ((8, PAD, 384), BF),
    ((8, PAD, 384), BF),
]


def local(sequence_acts, taps, dilations, left_link, projection, head_cotangent):
    hbm = pl.BlockSpec(memory_space=pltpu.HBM)
    results = (
        jax.ShapeDtypeStruct((1, C, ROWS), BF),
        jax.ShapeDtypeStruct((OWN, C), F32),
        jax.ShapeDtypeStruct((3, 2, C), F32),
    )
    parts = pl.pallas_call(
        kernel,
        out_shape=results,
        in_specs=[hbm] * 6,
        out_specs=(hbm, hbm, hbm),
        scratch_shapes=[pltpu.VMEM(shape, kind) for shape, kind in SCRATCH[:7]]
        + [pltpu.SMEM((2,), jnp.int32), pltpu.SMEM((1, SEQ), jnp.int32)]
        + [pltpu.VMEM(shape, kind) for shape, kind in SCRATCH[7:]]
        + [pltpu.SemaphoreType.DMA((44,)), pltpu.SemaphoreType.DMA((44,)), pltpu.SemaphoreType.DMA((6,)), pltpu.SemaphoreType.DMA((3,))],
        compiler_params=pltpu.CompilerParams(
            collective_id=0, has_side_effects=True, vmem_limit_bytes=60 * 1024 * 1024
        ),
        cost_estimate=pl.CostEstimate(
            flops=1_000_000_000, bytes_accessed=4_000_000, transcendentals=600_000
        ),
    )(sequence_acts, jnp.transpose(taps, (2, 0, 1)), dilations, left_link, projection, head_cotangent)
    grad, weight, tap_grads = pl.pallas_call(
        hand_over,
        out_shape=results,
        in_specs=[hbm] * 3,
        out_specs=(hbm,) * 3,
        scratch_shapes=[pltpu.VMEM(shape, kind) for shape, kind in SCRATCH[:3]]
        + [pltpu.SemaphoreType.DMA((6,))],
        compiler_params=pltpu.CompilerParams(vmem_limit_bytes=60 * 1024 * 1024),
    )(*parts)
    return grad, weight, jnp.transpose(tap_grads, (1, 2, 0))


def solution(mesh):
    placed = (P("dp", None, "seq"), P(), P(), P("dp", None), P("dp", None), P("dp", "seq", None))
    return jax.shard_map(
        local,
        mesh=mesh,
        in_specs=placed,
        out_specs=(P("dp", None, "seq"), P("seq", None), P()),
        check_vma=False,
    )
```

```python
import functools
import math

import jax
import jax.numpy as jnp
from jax import lax
from jax.experimental import pallas as pl
from jax.experimental.pallas import tpu as pltpu
from jax.sharding import PartitionSpec as P

MESH = pl.DeviceIdType.MESH
BF = jnp.bfloat16
F32 = jnp.float32

C = 768
ROWS = 256
HALF = 128
SEQ = 64
DP = 8
OWN = 14
PAD = 16
SLAB = 64
LAST_DILATION = 8
Z_PART, X_PART, SIB_PART = 32, 36, 40
FAR_FIRST = sorted(
    range(1, SEQ),
    key=lambda m: -100 * (m & 1) - ((0, 1, 2, 2)[m >> 4] + (0, 1, 2, 2, 4, 3, 2, 2)[(m >> 1) & 7]),
)
FAR_RING = (4, 3, 5, 2, 6, 1, 7)
GELU = 0.7978845608028654


def gelu_pair(v):
    th = jnp.tanh(GELU * (v + 0.044715 * v * v * v))
    act = 0.5 * v * (1.0 + th)
    slope = 0.5 * (1.0 + th) + 0.5 * v * (1.0 - th * th) * GELU * (1.0 + 3.0 * 0.044715 * v * v)
    return act, slope


def rounded(v):
    return v.astype(BF).astype(F32)


def earlier(tiles, lane, d):
    turned = [pltpu.roll(t, d, 1) for t in tiles]
    return [jnp.where(lane < d, turned[j - 1], turned[j]) for j in range(len(tiles))]


def later(tiles, lane, d):
    turned = [pltpu.roll(t, HALF - d, 1) for t in tiles]
    n = len(tiles)
    return [jnp.where(lane >= HALF - d, turned[(j + 1) % n], turned[j]) for j in range(n)]


def kernel(
    x_in, taps_in, dil_in, link_in, proj_in, cot_in,
    out_ref, pg_ref, tg_ref,
    x_ref, taps_ref, proj_ref, cot_ref, dil_ref, link_ref,
    stage, cot, cot_sib, pfull, edge_s, edge_r, cot_t, halo, wide,
    a0, a1, s0, s1, x2, pooled, pooled_sib, g2, g1, moved, prods, unit, halves, spread, matrix1, matrix0, pick_taps,
    a_s1, a_r1, a_s2, a_r2, a_s3, a_r3, a_r4, b_s1, b_r1, b_s2, b_r2, b_r3,
    t_r1, t_r2, t_r3,
    send, recv, load,
):
    s = lax.axis_index("seq")
    d = lax.axis_index("dp")
    core = s % 2
    y = (s // 2) % 8
    zl = s // 16
    x = d % 4
    zh = d // 4
    z8 = zh * 4 + zl
    sib = s + 1 - 2 * core

    def at_x(k):
        return {"seq": s, "dp": zh * 4 + (x + k) % 4}

    def at_x_core(xx, cc):
        return {"seq": s - core + cc, "dp": zh * 4 + xx}

    def at_y(yy):
        return {"seq": zl * 16 + yy * 2 + core, "dp": d}

    def at_z(zz):
        return {"seq": (zz % 4) * 16 + y * 2 + core, "dp": (zz // 4) * 4 + x}

    whole = {
        0: edge_s.at[0], 1: edge_s.at[0], 2: stage.at[pl.ds(0, 32)], 6: stage.at[pl.ds(0, 31)], 7: pooled, 12: cot_sib,
        13: b_r1.at[pl.ds(0, 7)], 14: a_r1.at[pl.ds(0, 3)], 21: cot_t.at[pl.ds(0, PAD)], 22: cot_t.at[pl.ds(0, PAD)],
        23: t_r1.at[pl.ds(0, 7)], 24: b_r2.at[pl.ds(0, 7)], 25: a_r2.at[pl.ds(0, 7)], 28: a_r3.at[pl.ds(0, 7)],
        26: t_r2.at[pl.ds(0, 7)], 27: b_r3.at[pl.ds(0, 3)],
        29: t_r3.at[pl.ds(0, 7)], 30: a_r4.at[pl.ds(0, 3)],
        3: pfull.at[0, pl.ds(0, 3)], 4: pfull.at[0, pl.ds(0, 4)],
    }
    for i in range(4):
        whole[Z_PART + i] = pfull.at[0, 0, pl.ds(0, PAD)]
        whole[X_PART + i] = pfull.at[0, pl.ds(0, 3), pl.ds(0, PAD)]
        whole[SIB_PART + i] = pfull.at[0, pl.ds(0, 4), pl.ds(0, PAD)]
    started, ended = [], []
    sibling = {"seq": sib, "dp": d}

    def push(src, dst, i, where):
        if i not in started:
            started.append(i)
        pltpu.make_async_remote_copy(
            src_ref=src, dst_ref=dst, send_sem=send.at[i], recv_sem=recv.at[i],
            device_id=where, device_id_type=MESH,
        ).start()

    def dummy(i):
        ref = whole[i]
        return pltpu.make_async_remote_copy(
            src_ref=ref, dst_ref=ref, send_sem=send.at[i], recv_sem=recv.at[i],
            device_id={"seq": sib, "dp": d}, device_id_type=MESH,
        )

    def arrived(i):
        ended.append(i)
        dummy(i).wait_recv()

    def finish():
        for i in started:
            if i not in ended:
                arrived(i)
            if i in range(Z_PART, Z_PART + 4):
                @pl.when((zl == 0) | (zl == 3))
                def _():
                    dummy(i).wait_send()
                    dummy(i).wait_send()
            else:
                dummy(i).wait_send()

    loads = [
        pltpu.make_async_copy(a, b, load.at[i])
        for i, (a, b) in enumerate(
            (
                (cot_in, cot_ref), (x_in, x_ref), (proj_in, proj_ref), (taps_in, taps_ref),
                (dil_in, dil_ref), (link_in, link_ref),
            )
        )
    ]
    barrier = pltpu.get_barrier_semaphore()

    def greet(where):
        pl.semaphore_signal(barrier, inc=1, device_id=where, device_id_type=MESH)

    @pl.loop(1, SEQ)
    def _(k):
        greet({"seq": (s + k) % SEQ, "dp": d})

    for k in range(4):
        greet({"seq": ((zl + k) % 4) * 16 + y * 2 + core, "dp": (1 - zh) * 4 + x})
    for k in range(1, 4):
        greet(at_x(k))
        greet({"seq": sib, "dp": zh * 4 + (x + k) % 4})

    for copy in loads:
        copy.start()

    lane = lax.broadcasted_iota(jnp.int32, (1, HALF), 1)

    def pack_edges(read, dst):
        for side in range(2):
            total = None
            for k in range(8):
                rows = pl.ds(96 * k, 96)
                part = read(1 - side, rows).astype(F32)
                part = pltpu.roll(part, (16 * k + 16 * (1 - side)) % HALF, 1)
                keep = (lane >= 16 * k) & (lane < 16 * k + 16)
                total = jnp.where(keep, part, 0.0 if total is None else total)
            dst[side] = total.astype(BF)

    def halo_keep(width):
        return ((lane < width) & right_linked) | ((lane >= HALF - width) & left_linked)

    def unpack_edges(src, dst):
        from_left = src[0].astype(F32)
        from_right = src[1].astype(F32)
        for k in range(8):
            left = pltpu.roll(from_left, (HALF - 16 - 16 * k) % HALF, 1)
            right = pltpu.roll(from_right, (HALF - 16 * k) % HALF, 1)
            tile = jnp.where(lane < HALF // 2, right, left)
            dst[pl.ds(96 * k, 96), :] = jnp.where(halo_keep(16), tile, 0.0)

    loads[0].wait()
    for t in range(SEQ):
        block = cot_ref[0, :, pl.ds(HALF * t, HALF)]
        stage[t] = jnp.concatenate(
            [block.astype(F32), jnp.zeros((PAD - OWN, HALF), F32)], axis=0
        ).astype(BF)

    loads[1].wait()
    pack_edges(lambda j, rows: x_ref[0, rows, pl.ds(HALF * j, HALF)], edge_s)

    loads[2].wait()
    row = lax.broadcasted_iota(jnp.int32, (64, 112), 0)
    col = lax.broadcasted_iota(jnp.int32, (64, 112), 1)
    inner = row % PAD
    source = OWN * (2 * (row // PAD) + core) + inner
    pick = jnp.where((inner < OWN) & (source == col), 1.0, 0.0).astype(BF)
    pfull[core, d] = jnp.dot(pick, proj_ref[...], preferred_element_type=F32).astype(BF)

    for copy in loads[3:]:
        copy.wait()
    left_linked = link_ref[0, s] >= 0
    right_linked = link_ref[0, (s + 1) % SEQ] >= 0
    six = jnp.concatenate([taps_ref[k] for k in range(3)] + [jnp.zeros((2, C), F32)], axis=0)
    six = jnp.transpose(six)
    for i in range(6):
        wide[i] = jnp.broadcast_to(six[:, i:i + 1], (C, HALF))
    d0 = dil_ref[0]


    unit[...] = jnp.where(
        lax.broadcasted_iota(jnp.int32, (HALF, HALF), 0) == lax.broadcasted_iota(jnp.int32, (HALF, HALF), 1),
        1.0, 0.0,
    ).astype(BF)
    two = lax.broadcasted_iota(jnp.int32, (ROWS, HALF), 0) // 2
    pair = two == lax.broadcasted_iota(jnp.int32, (ROWS, HALF), 1)
    halves[...] = jnp.where(pair, 0.5, 0.0).astype(BF)
    ring = 3 * HALF
    shape = (HALF + 2 * PAD, ring)
    at = lax.broadcasted_iota(jnp.int32, shape, 0)
    to = lax.broadcasted_iota(jnp.int32, shape, 1)
    right = (to >= ROWS) & (to < ROWS + 16) & right_linked
    left = (to >= ring - 16) & left_linked
    origin = jnp.where(
        to < ROWS, to // 2,
        jnp.where(right, HALF + (to - ROWS) // 2, jnp.where(left, HALF + 24 + (to - ring + 16) // 2, -1)),
    )
    spread[...] = jnp.where(at == origin, 1.0, 0.0).astype(BF)

    def shifts(dist, length):
        at = lax.broadcasted_iota(jnp.int32, (ring, 2 * length), 0)
        to = lax.broadcasted_iota(jnp.int32, (ring, 2 * length), 1)
        low = to < length
        to = jnp.where(low, to - dist + ring, to - length + dist)
        to = jnp.where(to >= ring, to - ring, to)
        return jnp.where(at == to, 1.0, 0.0).astype(BF)

    matrix1[...] = shifts(LAST_DILATION, ring)
    matrix0[...] = shifts(d0, ROWS)
    which = lax.broadcasted_iota(jnp.int32, (8, 12 * HALF), 1) // HALF
    row = lax.broadcasted_iota(jnp.int32, (8, 12 * HALF), 0)
    pick_taps[...] = jnp.where(which % 6 == row, 1.0, 0.0).astype(BF)

    pl.semaphore_wait(barrier, SEQ - 1 + 4 + 6)

    push(edge_s.at[0], edge_r.at[0], 0, {"seq": (s + 1) % SEQ, "dp": d})
    push(edge_s.at[1], edge_r.at[1], 1, {"seq": (s + SEQ - 1) % SEQ, "dp": d})
    for edge, step in ((0, -1), (3, 1)):
        @pl.when(zl == edge)
        def _():
            for i in range(4):
                rows = pfull.at[core, d, pl.ds(PAD * i, PAD)]
                for far in (2, 1):
                    push(rows, rows, Z_PART + i, at_z((z8 + 8 + far * step) % 8))
    me = core * 32 + zl * 8 + y
    for m in FAR_FIRST:
        t = s ^ m
        push(stage.at[t], cot.at[me], 2 if m & 1 else 6, {"seq": t, "dp": d})

    cot[me] = stage[s]

    for k in (2, 1, 3):
        push(pfull.at[core, d], pfull.at[core, d], 3, at_x(k))
    other = (1 - zh) * 4

    def pass_x(i):
        arrived(Z_PART + i)
        rows = pfull.at[core, other + x, pl.ds(PAD * i, PAD)]
        for k in (2, 1, 3):
            push(rows, rows, X_PART + i, at_x(k))

    def pass_core(i):
        arrived(X_PART + i)
        rows = pfull.at[core, pl.ds(other, 4), pl.ds(PAD * i, PAD)]
        push(rows, rows, SIB_PART + i, sibling)

    def weights(rows):
        return [[wide[2 * k + b, rows, :] for k in range(3)] for b in range(2)]

    @pl.loop(0, C // SLAB)
    def _(i):
        rows = pl.ds(pl.multiple_of(i * SLAB, SLAB), SLAB)
        for j in range(2):
            act, slope = gelu_pair(x_ref[0, rows, HALF * j:HALF * (j + 1)].astype(F32))
            a0[j, rows, :] = act
            s0[j, rows, :] = slope

    arrived(0)
    arrived(1)
    unpack_edges(edge_r, halo)

    def forward(first, last):
        @pl.loop(first, last)
        def _(i):
            rows = pl.ds(pl.multiple_of(i * SLAB, SLAB), SLAB)
            w = weights(rows)
            xs = [x_ref[0, rows, :HALF].astype(F32), x_ref[0, rows, HALF:].astype(F32), halo[rows, :]]
            acts = [a0[0, rows, :], a0[1, rows, :], gelu_pair(xs[2])[0]]
            lo, hi = earlier(acts, lane, d0), later(acts, lane, d0)
            ones = []
            acts1 = []
            for j in range(3):
                v = rounded(xs[j] + ((w[0][0] * lo[j] + w[0][1] * acts[j]) + w[0][2] * hi[j]))
                if j == 2:
                    v = jnp.where(halo_keep(8), v, 0.0)
                ones.append(v)
                act, slope = gelu_pair(v)
                acts1.append(act)
                if j < 2:
                    a1[j, rows, :] = act
                s1[j, rows, :] = slope
            lo, hi = earlier(acts1, lane, LAST_DILATION), later(acts1, lane, LAST_DILATION)
            for j in range(2):
                v = ones[j] + ((w[1][0] * lo[j] + w[1][1] * acts1[j]) + w[1][2] * hi[j])
                x2[rows, HALF * j:HALF * (j + 1)] = v.astype(BF)

    forward(0, 6)
    pass_x(0)
    pass_x(1)
    forward(6, 12)
    pooled[...] = jnp.dot(x2[...], halves[...], preferred_element_type=F32).astype(BF)
    push(pooled, pooled_sib, 7, {"seq": sib, "dp": d})
    pass_x(2)
    pass_x(3)
    arrived(2)
    push(cot.at[pl.ds((1 - core) * 32, 32)], cot_sib, 12, sibling)
    arrived(6)
    nt = (((1,), (1,)), ((), ()))
    cot_t[:HALF] = lax.dot_general(
        unit[...], cot[...].reshape(SEQ * PAD, HALF), nt,
        preferred_element_type=F32,
    ).astype(BF)
    push(cot_t.at[pl.ds(HALF - PAD, PAD)], cot_t.at[pl.ds(HALF + PAD, PAD)], 21, {"seq": (s + 1) % SEQ, "dp": d})
    push(cot_t.at[pl.ds(0, PAD)], cot_t.at[pl.ds(HALF, PAD)], 22, {"seq": (s + SEQ - 1) % SEQ, "dp": d})
    arrived(7)
    arrived(12)
    mine = cot[pl.ds(core * 32, 32)].reshape(512, HALF)
    theirs = cot_sib[...].reshape(512, HALF)
    for j in range(3):
        cols = pl.ds(256 * j, 256)
        part = lax.dot_general(mine, pooled[cols, :], nt, preferred_element_type=F32)
        part = part + lax.dot_general(theirs, pooled_sib[cols, :], nt, preferred_element_type=F32)
        part = part.astype(BF)
        if j == 2:
            b_s1[...] = part.reshape(4, 8, PAD, 256)
            for k in FAR_RING:
                yy = (y + k) % 8
                push(b_s1.at[:, yy], b_r1.at[y], 13, at_y(yy))
        else:
            a_s1[2 * j] = part[:, :HALF].reshape(4, 8, PAD, HALF)
            a_s1[2 * j + 1] = part[:, HALF:].reshape(4, 8, PAD, HALF)
        if j == 1:
            for k in (2, 1, 3):
                push(a_s1.at[(x + k) % 4], a_r1.at[x], 14, at_x(k))
    b_r1[y] = b_s1[:, y]
    a_r1[x] = a_s1[x]

    arrived(3)
    rows = pfull.at[core, pl.ds(zh * 4, 4)]
    push(rows, rows, 4, sibling)
    for i in range(4):
        pass_core(i)
    for i in (4, SIB_PART, SIB_PART + 1, SIB_PART + 2, SIB_PART + 3, 21, 22):
        arrived(i)
    back = jnp.dot(cot_t[...], pfull[...].reshape(SEQ * PAD, C), preferred_element_type=F32)
    back = (0.5 * back).astype(BF)
    g2[...] = lax.dot_general(
        back, spread[...], (((0,), (0,)), ((), ())), preferred_element_type=F32
    ).astype(BF)

    def keep_product(rows, column, total):
        high = total.astype(BF)
        prods[rows, HALF * column:HALF * (column + 1)] = high
        low = (total - high.astype(F32)).astype(BF)
        prods[rows, HALF * (column + 6):HALF * (column + 7)] = low

    moved[...] = jnp.dot(g2[...], matrix1[...], preferred_element_type=F32)

    @pl.loop(0, C // SLAB)
    def _(i):
        rows = pl.ds(pl.multiple_of(i * SLAB, SLAB), SLAB)
        w = weights(rows)[1]
        g = [g2[rows, HALF * j:HALF * (j + 1)].astype(F32) for j in range(3)]
        lo = [moved[rows, HALF * j:HALF * (j + 1)] for j in range(3)]
        hi = [moved[rows, ring + HALF * j:ring + HALF * (j + 1)] for j in range(3)]
        for j in range(3):
            conv = (w[0] * hi[j] + w[1] * g[j]) + w[2] * lo[j]
            v = g[j] + conv * s1[j, rows, :]
            if j == 2:
                v = jnp.where(halo_keep(8), v, 0.0)
            g1[rows, HALF * j:HALF * (j + 1)] = v.astype(BF)
        for k, part in enumerate((hi, g, lo)):
            keep_product(rows, 2 * k + 1, a1[0, rows, :] * part[0] + a1[1, rows, :] * part[1])

    moved[:, :2 * ROWS] = jnp.dot(g1[...], matrix0[...], preferred_element_type=F32)

    def around(rows):
        g = [g1[rows, HALF * j:HALF * (j + 1)].astype(F32) for j in range(2)]
        lo = [moved[rows, HALF * j:HALF * (j + 1)] for j in range(2)]
        hi = [moved[rows, ROWS + HALF * j:ROWS + HALF * (j + 1)] for j in range(2)]
        return hi, g, lo

    @pl.loop(0, C // SLAB)
    def _(i):
        rows = pl.ds(pl.multiple_of(i * SLAB, SLAB), SLAB)
        for k, part in enumerate(around(rows)):
            keep_product(rows, 2 * k, a0[0, rows, :] * part[0] + a0[1, rows, :] * part[1])

    flat = lax.dot_general(pick_taps[...], prods[...], nt, preferred_element_type=F32)
    slot = x * 2 + core
    t_r1[slot] = jnp.concatenate([flat[:, :384], flat[:, 384:]], axis=0).astype(BF)
    for k in (2, 1, 3, 0):
        for cc in range(2):
            if k:
                push(t_r1.at[slot], t_r1.at[slot], 23, at_x_core((x + k) % 4, cc))
    push(t_r1.at[slot], t_r1.at[slot], 23, sibling)

    @pl.loop(0, C // SLAB)
    def _(i):
        rows = pl.ds(pl.multiple_of(i * SLAB, SLAB), SLAB)
        w = weights(rows)[0]
        hi, g, lo = around(rows)
        for j in range(2):
            conv = (w[0] * hi[j] + w[1] * g[j]) + w[2] * lo[j]
            out_ref[0, rows, HALF * j:HALF * (j + 1)] = (g[j] + conv * s0[j, rows, :]).astype(BF)

    def total(ref):
        parts = [ref[i].astype(F32) for i in range(ref.shape[0])]
        while len(parts) > 1:
            parts = [a + b for a, b in zip(parts[::2], parts[1::2])]
        return parts[0]

    arrived(14)
    a_s2[...] = total(a_r1).astype(BF)
    for k in FAR_RING:
        yy = (y + k) % 8
        push(a_s2.at[:, yy], a_r2.at[y], 25, at_y(yy))
    a_r2[y] = a_s2[:, y]

    arrived(13)
    b_s2[...] = total(b_r1).astype(BF)
    for k in FAR_RING:
        zz = (z8 + k) % 8
        push(b_s2.at[zz % 4], b_r2.at[z8], 24, at_z(zz))
    b_r2[z8] = b_s2[zl]

    arrived(23)
    t_r2[z8] = total(t_r1).astype(BF)
    for k in FAR_RING:
        push(t_r2.at[z8], t_r2.at[z8], 26, at_z((z8 + k) % 8))

    arrived(25)
    a_s3[...] = total(a_r2).astype(BF)
    for k in FAR_RING:
        zz = (z8 + k) % 8
        push(a_s3.at[zz % 4], a_r3.at[z8], 28, at_z(zz))
    a_r3[z8] = a_s3[zl]

    arrived(24)
    b_r3[x] = total(b_r2)
    for k in (1, 3, 2):
        push(b_r3.at[x], b_r3.at[x], 27, at_x(k))

    arrived(26)
    t_r3[y] = total(t_r2).astype(BF)
    for k in FAR_RING:
        push(t_r3.at[y], t_r3.at[y], 29, at_y((y + k) % 8))

    arrived(28)
    a_r4[x] = total(a_r3)
    for k in (2, 1, 3):
        push(a_r4.at[x], a_r4.at[x], 30, at_x(k))

    arrived(29)
    taps_total = total(t_r3)

    scale = 1.0 / math.sqrt(SEQ * DP * HALF)
    arrived(27)
    pg_ref[:, 512:] = total(b_r3)[:OWN] * scale
    arrived(30)
    for j in range(4):
        pg_ref[:, HALF * j:HALF * (j + 1)] = a_r4[j][:OWN] * scale
    for h in range(2):
        for k in range(3):
            tg_ref[k, :, 384 * h:384 * (h + 1)] = taps_total[8 * h + 2 * k:8 * h + 2 * k + 2] * scale

    finish()


def hand_over(*refs):
    sems = refs[6]
    copies = [pltpu.make_async_copy(refs[i], refs[3 + i], sems.at[i]) for i in range(3)]
    for copy in copies:
        copy.start()
    for copy in copies:
        copy.wait()


SCRATCH = [
    ((1, C, ROWS), BF),
    ((3, 2, C), F32),
    ((112, C), BF),
    ((1, OWN, SEQ * HALF), BF),
    ((SEQ, PAD, HALF), BF),
    ((SEQ, PAD, HALF), BF),
    ((32, PAD, HALF), BF),
    ((2, DP, 64, C), BF),
    ((2, 96, HALF), BF),
    ((2, 96, HALF), BF),
    ((HALF + 2 * PAD, SEQ * PAD), BF),
    ((C, HALF), F32),
    ((6, C, HALF), F32),
    ((2, C, HALF), F32),
    ((2, C, HALF), F32),
    ((2, C, HALF), F32),
    ((3, C, HALF), F32),
    ((C, ROWS), BF),
    ((C, HALF), BF),
    ((C, HALF), BF),
    ((C, 3 * HALF), BF),
    ((C, 3 * HALF), BF),
    ((C, 6 * HALF), F32),
    ((C, 12 * HALF), BF),
    ((HALF, HALF), BF),
    ((ROWS, HALF), BF),
    ((HALF + 2 * PAD, 3 * HALF), BF),
    ((3 * HALF, 6 * HALF), BF),
    ((3 * HALF, 4 * HALF), BF),
    ((8, 12 * HALF), BF),
    ((4, 4, 8, PAD, HALF), BF),
    ((4, 4, 8, PAD, HALF), BF),
    ((4, 8, PAD, HALF), BF),
    ((8, 4, PAD, HALF), BF),
    ((4, PAD, HALF), BF),
    ((8, PAD, HALF), BF),
    ((4, PAD, HALF), F32),
    ((4, 8, PAD, 256), BF),
    ((8, 4, PAD, 256), BF),
    ((4, PAD, 256), BF),
    ((8, PAD, 256), BF),
    ((4, PAD, 256), F32),
    ((8, PAD, 384), BF),
    ((8, PAD, 384), BF),
    ((8, PAD, 384), BF),
]


def local(sequence_acts, taps, dilations, left_link, projection, head_cotangent):
    hbm = pl.BlockSpec(memory_space=pltpu.HBM)
    vmem = pl.BlockSpec(memory_space=pltpu.VMEM)
    results = (
        jax.ShapeDtypeStruct((1, C, ROWS), BF),
        jax.ShapeDtypeStruct((OWN, C), F32),
        jax.ShapeDtypeStruct((3, 2, C), F32),
    )
    parts = pl.pallas_call(
        kernel,
        out_shape=tuple(pltpu.VMEM(r.shape, r.dtype) for r in results),
        in_specs=[hbm] * 6,
        out_specs=(vmem,) * 3,
        scratch_shapes=[pltpu.VMEM(shape, kind) for shape, kind in SCRATCH[:4]]
        + [pltpu.SMEM((2,), jnp.int32), pltpu.SMEM((1, SEQ), jnp.int32)]
        + [pltpu.VMEM(shape, kind) for shape, kind in SCRATCH[4:]]
        + [pltpu.SemaphoreType.DMA((44,)), pltpu.SemaphoreType.DMA((44,)), pltpu.SemaphoreType.DMA((6,))],
        compiler_params=pltpu.CompilerParams(
            collective_id=0, has_side_effects=True, vmem_limit_bytes=60 * 1024 * 1024
        ),
        cost_estimate=pl.CostEstimate(
            flops=1_000_000_000, bytes_accessed=4_000_000, transcendentals=600_000
        ),
    )(sequence_acts, jnp.transpose(taps, (2, 0, 1)), dilations, left_link, projection, head_cotangent)
    grad, weight, tap_grads = pl.pallas_call(
        hand_over,
        out_shape=results,
        in_specs=[vmem] * 3,
        out_specs=(hbm,) * 3,
        scratch_shapes=[pltpu.SemaphoreType.DMA((3,))],
        compiler_params=pltpu.CompilerParams(vmem_limit_bytes=16 * 1024 * 1024),
    )(*parts)
    return grad, weight, jnp.transpose(tap_grads, (1, 2, 0))


def solution(mesh):
    placed = (P("dp", None, "seq"), P(), P(), P("dp", None), P("dp", None), P("dp", "seq", None))
    return jax.shard_map(
        local,
        mesh=mesh,
        in_specs=placed,
        out_specs=(P("dp", None, "seq"), P("seq", None), P()),
        check_vma=False,
    )
```

```python
import functools
import math

import jax
import jax.numpy as jnp
from jax import lax
from jax.experimental import pallas as pl
from jax.experimental.pallas import tpu as pltpu
from jax.sharding import PartitionSpec as P

MESH = pl.DeviceIdType.MESH
BF = jnp.bfloat16
F32 = jnp.float32

C = 768
ROWS = 256
HALF = 128
SEQ = 64
DP = 8
OWN = 14
PAD = 16
SLAB = 64
LAST_DILATION = 8
Z_PART, X_PART, SIB_PART, A_X, A_Y = 32, 36, 40, 44, 46
FAR_FIRST = sorted(
    range(1, SEQ),
    key=lambda m: -100 * (m & 1) - ((0, 1, 2, 2)[m >> 4] + (0, 1, 2, 2, 4, 3, 2, 2)[(m >> 1) & 7]),
)
FAR_RING = (4, 3, 5, 2, 6, 1, 7)
GELU = 0.7978845608028654


def gelu_pair(v):
    th = jnp.tanh(GELU * (v + 0.044715 * v * v * v))
    act = 0.5 * v * (1.0 + th)
    slope = 0.5 * (1.0 + th) + 0.5 * v * (1.0 - th * th) * GELU * (1.0 + 3.0 * 0.044715 * v * v)
    return act, slope


def rounded(v):
    return v.astype(BF).astype(F32)


def earlier(tiles, lane, d):
    turned = [pltpu.roll(t, d, 1) for t in tiles]
    return [jnp.where(lane < d, turned[j - 1], turned[j]) for j in range(len(tiles))]


def later(tiles, lane, d):
    turned = [pltpu.roll(t, HALF - d, 1) for t in tiles]
    n = len(tiles)
    return [jnp.where(lane >= HALF - d, turned[(j + 1) % n], turned[j]) for j in range(n)]


def kernel(
    x_in, taps_in, dil_in, link_in, proj_in, cot_in,
    out_ref, pg_ref, tg_ref,
    x_ref, taps_ref, proj_ref, cot_ref, dil_ref, link_ref,
    stage, cot, cot_sib, pfull, edge_s, edge_r, cot_t, halo, wide,
    a0, a1, s0, s1, x2, pooled, pooled_sib, g2, g1, moved, prods, unit, halves, spread, matrix1, matrix0, pick_taps,
    a_s1, a_r1, a_s2, a_r2, a_s3, a_r3, a_r4, b_s1, b_r1, b_s2, b_r2, b_r3,
    t_r1, t_r2, t_r3, t_f,
    send, recv, load,
):
    s = lax.axis_index("seq")
    d = lax.axis_index("dp")
    core = s % 2
    y = (s // 2) % 8
    zl = s // 16
    x = d % 4
    zh = d // 4
    z8 = zh * 4 + zl
    sib = s + 1 - 2 * core

    def at_x(k):
        return {"seq": s, "dp": zh * 4 + (x + k) % 4}

    def at_x_core(xx, cc):
        return {"seq": s - core + cc, "dp": zh * 4 + xx}

    def at_y(yy):
        return {"seq": zl * 16 + yy * 2 + core, "dp": d}

    def at_z(zz):
        return {"seq": (zz % 4) * 16 + y * 2 + core, "dp": (zz // 4) * 4 + x}

    whole = {
        0: edge_s.at[0], 1: edge_s.at[0], 2: stage.at[pl.ds(0, 32)], 6: stage.at[pl.ds(0, 31)], 7: pooled, 12: cot_sib,
        13: b_r1.at[pl.ds(0, 7)], 21: cot_t.at[pl.ds(0, PAD)], 22: cot_t.at[pl.ds(0, PAD)],
        23: t_r1.at[pl.ds(0, 7)], 24: b_r2.at[pl.ds(0, 7)], 28: a_r3.at[pl.ds(0, 7)],
        26: t_r2.at[pl.ds(0, 7)], 27: b_r3.at[pl.ds(0, 3)],
        29: t_r3.at[pl.ds(0, 7)], 31: t_f, 30: a_r4.at[pl.ds(0, 3)],
        3: pfull.at[0, pl.ds(0, 3)], 4: pfull.at[0, pl.ds(0, 4)],
    }
    for h in range(2):
        whole[A_X + h] = a_r1.at[pl.ds(0, 3), pl.ds(0, 2)]
        whole[A_Y + h] = a_r2.at[pl.ds(0, 7), pl.ds(0, 2)]
    for i in range(4):
        whole[Z_PART + i] = pfull.at[0, 0, pl.ds(0, PAD)]
        whole[X_PART + i] = pfull.at[0, pl.ds(0, 3), pl.ds(0, PAD)]
        whole[SIB_PART + i] = pfull.at[0, pl.ds(0, 4), pl.ds(0, PAD)]
    started, ended = [], []
    sibling = {"seq": sib, "dp": d}

    def push(src, dst, i, where):
        if i not in started:
            started.append(i)
        pltpu.make_async_remote_copy(
            src_ref=src, dst_ref=dst, send_sem=send.at[i], recv_sem=recv.at[i],
            device_id=where, device_id_type=MESH,
        ).start()

    def dummy(i):
        ref = whole[i]
        return pltpu.make_async_remote_copy(
            src_ref=ref, dst_ref=ref, send_sem=send.at[i], recv_sem=recv.at[i],
            device_id={"seq": sib, "dp": d}, device_id_type=MESH,
        )

    def arrived(i):
        ended.append(i)
        dummy(i).wait_recv()

    def on_core(c):
        return pl.when(core == c)

    def finish():
        for i in started:
            if i not in ended:
                arrived(i)
            if i == 23:
                for c in range(2):
                    @on_core(c)
                    def _():
                        block = t_r1.at[pl.ds(0, 4 - c)]
                        pltpu.make_async_remote_copy(
                            src_ref=block, dst_ref=block, send_sem=send.at[i], recv_sem=recv.at[i],
                            device_id=sibling, device_id_type=MESH,
                        ).wait_send()
            elif i in (26, 29, 31):
                @on_core(1)
                def _():
                    dummy(i).wait_send()
            elif i in range(Z_PART, Z_PART + 4):
                @pl.when((zl == 0) | (zl == 3))
                def _():
                    dummy(i).wait_send()
                    dummy(i).wait_send()
            else:
                dummy(i).wait_send()

    loads = [
        pltpu.make_async_copy(a, b, load.at[i])
        for i, (a, b) in enumerate(
            (
                (cot_in, cot_ref), (x_in, x_ref), (proj_in, proj_ref), (taps_in, taps_ref),
                (dil_in, dil_ref), (link_in, link_ref),
            )
        )
    ]
    barrier = pltpu.get_barrier_semaphore()

    def greet(where):
        pl.semaphore_signal(barrier, inc=1, device_id=where, device_id_type=MESH)

    @pl.loop(1, SEQ)
    def _(k):
        greet({"seq": (s + k) % SEQ, "dp": d})

    for k in range(4):
        greet({"seq": ((zl + k) % 4) * 16 + y * 2 + core, "dp": (1 - zh) * 4 + x})
    for k in range(1, 4):
        greet(at_x(k))
        greet({"seq": sib, "dp": zh * 4 + (x + k) % 4})

    for copy in loads:
        copy.start()

    lane = lax.broadcasted_iota(jnp.int32, (1, HALF), 1)

    def pack_edges(read, dst):
        for side in range(2):
            total = None
            for k in range(8):
                rows = pl.ds(96 * k, 96)
                part = read(1 - side, rows).astype(F32)
                part = pltpu.roll(part, (16 * k + 16 * (1 - side)) % HALF, 1)
                keep = (lane >= 16 * k) & (lane < 16 * k + 16)
                total = jnp.where(keep, part, 0.0 if total is None else total)
            dst[side] = total.astype(BF)

    def halo_keep(width):
        return ((lane < width) & right_linked) | ((lane >= HALF - width) & left_linked)

    def unpack_edges(src, dst):
        from_left = src[0].astype(F32)
        from_right = src[1].astype(F32)
        for k in range(8):
            left = pltpu.roll(from_left, (HALF - 16 - 16 * k) % HALF, 1)
            right = pltpu.roll(from_right, (HALF - 16 * k) % HALF, 1)
            tile = jnp.where(lane < HALF // 2, right, left)
            dst[pl.ds(96 * k, 96), :] = jnp.where(halo_keep(16), tile, 0.0)

    loads[0].wait()
    for t in range(SEQ):
        block = cot_ref[0, :, pl.ds(HALF * t, HALF)]
        stage[t] = jnp.concatenate(
            [block.astype(F32), jnp.zeros((PAD - OWN, HALF), F32)], axis=0
        ).astype(BF)

    loads[1].wait()
    pack_edges(lambda j, rows: x_ref[0, rows, pl.ds(HALF * j, HALF)], edge_s)

    loads[2].wait()
    row = lax.broadcasted_iota(jnp.int32, (64, 112), 0)
    col = lax.broadcasted_iota(jnp.int32, (64, 112), 1)
    inner = row % PAD
    source = OWN * (2 * (row // PAD) + core) + inner
    pick = jnp.where((inner < OWN) & (source == col), 1.0, 0.0).astype(BF)
    pfull[core, d] = jnp.dot(pick, proj_ref[...], preferred_element_type=F32).astype(BF)

    for copy in loads[3:]:
        copy.wait()
    left_linked = link_ref[0, s] >= 0
    right_linked = link_ref[0, (s + 1) % SEQ] >= 0
    six = jnp.concatenate([taps_ref[k] for k in range(3)] + [jnp.zeros((2, C), F32)], axis=0)
    six = jnp.transpose(six)
    for i in range(6):
        wide[i] = jnp.broadcast_to(six[:, i:i + 1], (C, HALF))
    d0 = dil_ref[0]


    unit[...] = jnp.where(
        lax.broadcasted_iota(jnp.int32, (HALF, HALF), 0) == lax.broadcasted_iota(jnp.int32, (HALF, HALF), 1),
        1.0, 0.0,
    ).astype(BF)
    two = lax.broadcasted_iota(jnp.int32, (ROWS, HALF), 0) // 2
    pair = two == lax.broadcasted_iota(jnp.int32, (ROWS, HALF), 1)
    halves[...] = jnp.where(pair, 0.5, 0.0).astype(BF)
    ring = 3 * HALF
    shape = (HALF + 2 * PAD, ring)
    at = lax.broadcasted_iota(jnp.int32, shape, 0)
    to = lax.broadcasted_iota(jnp.int32, shape, 1)
    right = (to >= ROWS) & (to < ROWS + 16) & right_linked
    left = (to >= ring - 16) & left_linked
    origin = jnp.where(
        to < ROWS, to // 2,
        jnp.where(right, HALF + (to - ROWS) // 2, jnp.where(left, HALF + 24 + (to - ring + 16) // 2, -1)),
    )
    spread[...] = jnp.where(at == origin, 1.0, 0.0).astype(BF)

    def shifts(dist, length):
        at = lax.broadcasted_iota(jnp.int32, (ring, 2 * length), 0)
        to = lax.broadcasted_iota(jnp.int32, (ring, 2 * length), 1)
        low = to < length
        to = jnp.where(low, to - dist + ring, to - length + dist)
        to = jnp.where(to >= ring, to - ring, to)
        return jnp.where(at == to, 1.0, 0.0).astype(BF)

    matrix1[...] = shifts(LAST_DILATION, ring)
    matrix0[...] = shifts(d0, ROWS)
    which = lax.broadcasted_iota(jnp.int32, (8, 12 * HALF), 1) // HALF
    row = lax.broadcasted_iota(jnp.int32, (8, 12 * HALF), 0)
    pick_taps[...] = jnp.where(which % 6 == row, 1.0, 0.0).astype(BF)

    pl.semaphore_wait(barrier, SEQ - 1 + 4 + 6)

    push(edge_s.at[0], edge_r.at[0], 0, {"seq": (s + 1) % SEQ, "dp": d})
    push(edge_s.at[1], edge_r.at[1], 1, {"seq": (s + SEQ - 1) % SEQ, "dp": d})
    for edge, step in ((0, -1), (3, 1)):
        @pl.when(zl == edge)
        def _():
            for i in range(4):
                rows = pfull.at[core, d, pl.ds(PAD * i, PAD)]
                for far in (2, 1):
                    push(rows, rows, Z_PART + i, at_z((z8 + 8 + far * step) % 8))
    me = core * 32 + zl * 8 + y
    for m in FAR_FIRST:
        t = s ^ m
        push(stage.at[t], cot.at[me], 2 if m & 1 else 6, {"seq": t, "dp": d})

    cot[me] = stage[s]

    for k in (2, 1, 3):
        push(pfull.at[core, d], pfull.at[core, d], 3, at_x(k))
    other = (1 - zh) * 4

    def pass_x(i):
        arrived(Z_PART + i)
        rows = pfull.at[core, other + x, pl.ds(PAD * i, PAD)]
        for k in (2, 1, 3):
            push(rows, rows, X_PART + i, at_x(k))

    def pass_core(i):
        arrived(X_PART + i)
        rows = pfull.at[core, pl.ds(other, 4), pl.ds(PAD * i, PAD)]
        push(rows, rows, SIB_PART + i, sibling)

    def weights(rows):
        return [[wide[2 * k + b, rows, :] for k in range(3)] for b in range(2)]

    @pl.loop(0, C // SLAB)
    def _(i):
        rows = pl.ds(pl.multiple_of(i * SLAB, SLAB), SLAB)
        for j in range(2):
            act, slope = gelu_pair(x_ref[0, rows, HALF * j:HALF * (j + 1)].astype(F32))
            a0[j, rows, :] = act
            s0[j, rows, :] = slope

    arrived(0)
    arrived(1)
    unpack_edges(edge_r, halo)

    def forward(first, last):
        @pl.loop(first, last)
        def _(i):
            rows = pl.ds(pl.multiple_of(i * SLAB, SLAB), SLAB)
            w = weights(rows)
            xs = [x_ref[0, rows, :HALF].astype(F32), x_ref[0, rows, HALF:].astype(F32), halo[rows, :]]
            acts = [a0[0, rows, :], a0[1, rows, :], gelu_pair(xs[2])[0]]
            lo, hi = earlier(acts, lane, d0), later(acts, lane, d0)
            ones = []
            acts1 = []
            for j in range(3):
                v = rounded(xs[j] + ((w[0][0] * lo[j] + w[0][1] * acts[j]) + w[0][2] * hi[j]))
                if j == 2:
                    v = jnp.where(halo_keep(8), v, 0.0)
                ones.append(v)
                act, slope = gelu_pair(v)
                acts1.append(act)
                if j < 2:
                    a1[j, rows, :] = act
                s1[j, rows, :] = slope
            lo, hi = earlier(acts1, lane, LAST_DILATION), later(acts1, lane, LAST_DILATION)
            for j in range(2):
                v = ones[j] + ((w[1][0] * lo[j] + w[1][1] * acts1[j]) + w[1][2] * hi[j])
                x2[rows, HALF * j:HALF * (j + 1)] = v.astype(BF)

    forward(0, 6)
    pass_x(0)
    pass_x(1)
    forward(6, 12)
    pooled[...] = jnp.dot(x2[...], halves[...], preferred_element_type=F32).astype(BF)
    push(pooled, pooled_sib, 7, {"seq": sib, "dp": d})
    pass_x(2)
    pass_x(3)
    arrived(2)
    push(cot.at[pl.ds((1 - core) * 32, 32)], cot_sib, 12, sibling)
    arrived(6)
    nt = (((1,), (1,)), ((), ()))
    cot_t[:HALF] = lax.dot_general(
        unit[...], cot[...].reshape(SEQ * PAD, HALF), nt,
        preferred_element_type=F32,
    ).astype(BF)
    push(cot_t.at[pl.ds(HALF - PAD, PAD)], cot_t.at[pl.ds(HALF + PAD, PAD)], 21, {"seq": (s + 1) % SEQ, "dp": d})
    push(cot_t.at[pl.ds(0, PAD)], cot_t.at[pl.ds(HALF, PAD)], 22, {"seq": (s + SEQ - 1) % SEQ, "dp": d})
    arrived(7)
    arrived(12)
    mine = cot[pl.ds(core * 32, 32)].reshape(512, HALF)
    theirs = cot_sib[...].reshape(512, HALF)
    for j in range(3):
        cols = pl.ds(256 * j, 256)
        part = lax.dot_general(mine, pooled[cols, :], nt, preferred_element_type=F32)
        part = part + lax.dot_general(theirs, pooled_sib[cols, :], nt, preferred_element_type=F32)
        part = part.astype(BF)
        if j == 2:
            b_s1[...] = part.reshape(4, 8, PAD, 256)
            for k in FAR_RING:
                yy = (y + k) % 8
                push(b_s1.at[:, yy], b_r1.at[y], 13, at_y(yy))
        else:
            a_s1[2 * j] = part[:, :HALF].reshape(4, 8, PAD, HALF)
            a_s1[2 * j + 1] = part[:, HALF:].reshape(4, 8, PAD, HALF)
        if j == 1:
            for h in range(2):
                part_z = pl.ds(2 * h, 2)
                for k in (2, 1, 3):
                    push(a_s1.at[(x + k) % 4, part_z], a_r1.at[x, part_z], A_X + h, at_x(k))
    b_r1[y] = b_s1[:, y]
    a_r1[x] = a_s1[x]

    def total(ref):
        parts = [ref[i].astype(F32) for i in range(ref.shape[0])]
        while len(parts) > 1:
            parts = [a + b for a, b in zip(parts[::2], parts[1::2])]
        return parts[0]

    def weight_y(h):
        part_z = pl.ds(2 * h, 2)
        arrived(A_X + h)
        a_s2[part_z] = total(a_r1.at[:, part_z]).astype(BF)
        for k in FAR_RING:
            yy = (y + k) % 8
            push(a_s2.at[part_z, yy], a_r2.at[y, part_z], A_Y + h, at_y(yy))

    arrived(3)
    rows = pfull.at[core, pl.ds(zh * 4, 4)]
    push(rows, rows, 4, sibling)
    for i in range(4):
        pass_core(i)
    for i in (4, SIB_PART, SIB_PART + 1, SIB_PART + 2, SIB_PART + 3, 21, 22):
        arrived(i)
    back = jnp.dot(cot_t[...], pfull[...].reshape(SEQ * PAD, C), preferred_element_type=F32)
    back = (0.5 * back).astype(BF)
    g2[...] = lax.dot_general(
        back, spread[...], (((0,), (0,)), ((), ())), preferred_element_type=F32
    ).astype(BF)

    def keep_product(rows, column, total):
        high = total.astype(BF)
        prods[rows, HALF * column:HALF * (column + 1)] = high
        low = (total - high.astype(F32)).astype(BF)
        prods[rows, HALF * (column + 6):HALF * (column + 7)] = low

    moved[...] = jnp.dot(g2[...], matrix1[...], preferred_element_type=F32)

    @pl.loop(0, C // SLAB)
    def _(i):
        rows = pl.ds(pl.multiple_of(i * SLAB, SLAB), SLAB)
        w = weights(rows)[1]
        g = [g2[rows, HALF * j:HALF * (j + 1)].astype(F32) for j in range(3)]
        lo = [moved[rows, HALF * j:HALF * (j + 1)] for j in range(3)]
        hi = [moved[rows, ring + HALF * j:ring + HALF * (j + 1)] for j in range(3)]
        for j in range(3):
            conv = (w[0] * hi[j] + w[1] * g[j]) + w[2] * lo[j]
            v = g[j] + conv * s1[j, rows, :]
            if j == 2:
                v = jnp.where(halo_keep(8), v, 0.0)
            g1[rows, HALF * j:HALF * (j + 1)] = v.astype(BF)
        for k, part in enumerate((hi, g, lo)):
            keep_product(rows, 2 * k + 1, a1[0, rows, :] * part[0] + a1[1, rows, :] * part[1])

    weight_y(0)
    moved[:, :2 * ROWS] = jnp.dot(g1[...], matrix0[...], preferred_element_type=F32)

    def around(rows):
        g = [g1[rows, HALF * j:HALF * (j + 1)].astype(F32) for j in range(2)]
        lo = [moved[rows, HALF * j:HALF * (j + 1)] for j in range(2)]
        hi = [moved[rows, ROWS + HALF * j:ROWS + HALF * (j + 1)] for j in range(2)]
        return hi, g, lo

    @pl.loop(0, C // SLAB)
    def _(i):
        rows = pl.ds(pl.multiple_of(i * SLAB, SLAB), SLAB)
        for k, part in enumerate(around(rows)):
            keep_product(rows, 2 * k, a0[0, rows, :] * part[0] + a0[1, rows, :] * part[1])

    flat = lax.dot_general(pick_taps[...], prods[...], nt, preferred_element_type=F32)
    slot = x * 2 + core
    t_r1[slot] = jnp.concatenate([flat[:, :384], flat[:, 384:]], axis=0).astype(BF)
    for k in (2, 1, 3):
        push(t_r1.at[slot], t_r1.at[slot], 23, at_x_core((x + k) % 4, 1))

    @on_core(0)
    def _():
        push(t_r1.at[slot], t_r1.at[slot], 23, sibling)

    def push_unless(zz, src):
        @pl.when(zz != z8)
        def _():
            push(src, a_r3.at[z8], 28, at_z(zz))

    weight_y(1)
    a_r2[y] = a_s2[:, y]

    arrived(13)
    b_s2[...] = total(b_r1).astype(BF)
    for k in FAR_RING:
        zz = (z8 + k) % 8
        push(b_s2.at[zz % 4], b_r2.at[z8], 24, at_z(zz))
    b_r2[z8] = b_s2[zl]

    @pl.loop(0, C // SLAB)
    def _(i):
        rows = pl.ds(pl.multiple_of(i * SLAB, SLAB), SLAB)
        w = weights(rows)[0]
        hi, g, lo = around(rows)
        for j in range(2):
            conv = (w[0] * hi[j] + w[1] * g[j]) + w[2] * lo[j]
            out_ref[0, rows, HALF * j:HALF * (j + 1)] = (g[j] + conv * s0[j, rows, :]).astype(BF)

    @on_core(1)
    def _():
        arrived(23)
        t_r2[z8] = total(t_r1).astype(BF)
        for k in FAR_RING:
            push(t_r2.at[z8], t_r2.at[z8], 26, at_z((z8 + k) % 8))

    for h in range(2):
        part_z = pl.ds(2 * h, 2)
        arrived(A_Y + h)
        a_s3[part_z] = total(a_r2.at[:, part_z]).astype(BF)
        for low in (2 * h, 2 * h + 1):
            for high in (0, 4):
                push_unless(high + low, a_s3.at[low])
    a_r3[z8] = a_s3[zl]

    arrived(24)
    b_r3[x] = total(b_r2)
    for k in (1, 3, 2):
        push(b_r3.at[x], b_r3.at[x], 27, at_x(k))

    @on_core(1)
    def _():
        arrived(26)
        t_r3[y] = total(t_r2).astype(BF)
        for k in FAR_RING:
            push(t_r3.at[y], t_r3.at[y], 29, at_y((y + k) % 8))

    arrived(28)
    a_r4[x] = total(a_r3)
    for k in (2, 1, 3):
        push(a_r4.at[x], a_r4.at[x], 30, at_x(k))

    @on_core(1)
    def _():
        arrived(29)
        t_f[...] = total(t_r3)
        push(t_f, t_f, 31, sibling)

    scale = 1.0 / math.sqrt(SEQ * DP * HALF)
    arrived(27)
    pg_ref[:, 512:] = total(b_r3)[:OWN] * scale
    arrived(30)
    for j in range(4):
        pg_ref[:, HALF * j:HALF * (j + 1)] = a_r4[j][:OWN] * scale
    @on_core(0)
    def _():
        arrived(31)

    taps_total = t_f[...]
    for h in range(2):
        for k in range(3):
            tg_ref[k, :, 384 * h:384 * (h + 1)] = taps_total[8 * h + 2 * k:8 * h + 2 * k + 2] * scale

    finish()


def hand_over(*refs):
    sems = refs[6]
    copies = [pltpu.make_async_copy(refs[i], refs[3 + i], sems.at[i]) for i in range(3)]
    for copy in copies:
        copy.start()
    for copy in copies:
        copy.wait()


SCRATCH = [
    ((1, C, ROWS), BF),
    ((3, 2, C), F32),
    ((112, C), BF),
    ((1, OWN, SEQ * HALF), BF),
    ((SEQ, PAD, HALF), BF),
    ((SEQ, PAD, HALF), BF),
    ((32, PAD, HALF), BF),
    ((2, DP, 64, C), BF),
    ((2, 96, HALF), BF),
    ((2, 96, HALF), BF),
    ((HALF + 2 * PAD, SEQ * PAD), BF),
    ((C, HALF), F32),
    ((6, C, HALF), F32),
    ((2, C, HALF), F32),
    ((2, C, HALF), F32),
    ((2, C, HALF), F32),
    ((3, C, HALF), F32),
    ((C, ROWS), BF),
    ((C, HALF), BF),
    ((C, HALF), BF),
    ((C, 3 * HALF), BF),
    ((C, 3 * HALF), BF),
    ((C, 6 * HALF), F32),
    ((C, 12 * HALF), BF),
    ((HALF, HALF), BF),
    ((ROWS, HALF), BF),
    ((HALF + 2 * PAD, 3 * HALF), BF),
    ((3 * HALF, 6 * HALF), BF),
    ((3 * HALF, 4 * HALF), BF),
    ((8, 12 * HALF), BF),
    ((4, 4, 8, PAD, HALF), BF),
    ((4, 4, 8, PAD, HALF), BF),
    ((4, 8, PAD, HALF), BF),
    ((8, 4, PAD, HALF), BF),
    ((4, PAD, HALF), BF),
    ((8, PAD, HALF), BF),
    ((4, PAD, HALF), F32),
    ((4, 8, PAD, 256), BF),
    ((8, 4, PAD, 256), BF),
    ((4, PAD, 256), BF),
    ((8, PAD, 256), BF),
    ((4, PAD, 256), F32),
    ((8, PAD, 384), BF),
    ((8, PAD, 384), BF),
    ((8, PAD, 384), BF),
    ((PAD, 384), F32),
]


def local(sequence_acts, taps, dilations, left_link, projection, head_cotangent):
    hbm = pl.BlockSpec(memory_space=pltpu.HBM)
    vmem = pl.BlockSpec(memory_space=pltpu.VMEM)
    results = (
        jax.ShapeDtypeStruct((1, C, ROWS), BF),
        jax.ShapeDtypeStruct((OWN, C), F32),
        jax.ShapeDtypeStruct((3, 2, C), F32),
    )
    parts = pl.pallas_call(
        kernel,
        out_shape=tuple(pltpu.VMEM(r.shape, r.dtype) for r in results),
        in_specs=[hbm] * 6,
        out_specs=(vmem,) * 3,
        scratch_shapes=[pltpu.VMEM(shape, kind) for shape, kind in SCRATCH[:4]]
        + [pltpu.SMEM((2,), jnp.int32), pltpu.SMEM((1, SEQ), jnp.int32)]
        + [pltpu.VMEM(shape, kind) for shape, kind in SCRATCH[4:]]
        + [pltpu.SemaphoreType.DMA((48,)), pltpu.SemaphoreType.DMA((48,)), pltpu.SemaphoreType.DMA((6,))],
        compiler_params=pltpu.CompilerParams(
            collective_id=0, has_side_effects=True, vmem_limit_bytes=60 * 1024 * 1024
        ),
        cost_estimate=pl.CostEstimate(
            flops=1_000_000_000, bytes_accessed=4_000_000, transcendentals=600_000
        ),
    )(sequence_acts, jnp.transpose(taps, (2, 0, 1)), dilations, left_link, projection, head_cotangent)
    grad, weight, tap_grads = pl.pallas_call(
        hand_over,
        out_shape=results,
        in_specs=[vmem] * 3,
        out_specs=(hbm,) * 3,
        scratch_shapes=[pltpu.SemaphoreType.DMA((3,))],
        compiler_params=pltpu.CompilerParams(vmem_limit_bytes=16 * 1024 * 1024),
    )(*parts)
    return grad, weight, jnp.transpose(tap_grads, (1, 2, 0))


def solution(mesh):
    placed = (P("dp", None, "seq"), P(), P(), P("dp", None), P("dp", None), P("dp", "seq", None))
    return jax.shard_map(
        local,
        mesh=mesh,
        in_specs=placed,
        out_specs=(P("dp", None, "seq"), P("seq", None), P()),
        check_vma=False,
    )
```

```python
import functools
import math

import jax
import jax.numpy as jnp
from jax import lax
from jax.experimental import pallas as pl
from jax.experimental.pallas import tpu as pltpu
from jax.sharding import PartitionSpec as P

MESH = pl.DeviceIdType.MESH
BF = jnp.bfloat16
F32 = jnp.float32

C = 768
ROWS = 256
HALF = 128
SEQ = 64
DP = 8
OWN = 14
PAD = 16
SLAB = 64
LAST_DILATION = 8
Z_PART, X_PART, SIB_PART, A_X, A_Y = 32, 36, 40, 44, 46
FAR_FIRST = sorted(
    range(1, SEQ),
    key=lambda m: -100 * (m & 1) - ((0, 1, 2, 2)[m >> 4] + (0, 1, 2, 2, 4, 3, 2, 2)[(m >> 1) & 7]),
)
FAR_RING = (4, 3, 5, 2, 6, 1, 7)
GELU = 0.7978845608028654


def gelu_pair(v):
    th = jnp.tanh(GELU * (v + 0.044715 * v * v * v))
    act = 0.5 * v * (1.0 + th)
    slope = 0.5 * (1.0 + th) + 0.5 * v * (1.0 - th * th) * GELU * (1.0 + 3.0 * 0.044715 * v * v)
    return act, slope


def rounded(v):
    return v.astype(BF).astype(F32)


def earlier(tiles, lane, d):
    turned = [pltpu.roll(t, d, 1) for t in tiles]
    return [jnp.where(lane < d, turned[j - 1], turned[j]) for j in range(len(tiles))]


def later(tiles, lane, d):
    turned = [pltpu.roll(t, HALF - d, 1) for t in tiles]
    n = len(tiles)
    return [jnp.where(lane >= HALF - d, turned[(j + 1) % n], turned[j]) for j in range(n)]


def kernel(
    x_ref, taps_in, dil_in, link_in, proj_ref, cot_ref,
    out_ref, pg_ref, tg_ref,
    taps_ref, dil_ref, link_ref,
    stage, cot, cot_sib, pfull, edge_s, edge_r, cot_t, halo, wide,
    a0, a1, s0, s1, x2, pooled, pooled_sib, g2, g1, moved, prods, unit, halves, spread, matrix1, matrix0, pick_taps,
    a_s1, a_r1, a_s2, a_r2, a_s3, a_r3, a_r4, b_s1, b_r1, b_s2, b_r2, b_r3,
    t_r1, t_r2, t_r3, t_f,
    send, recv, load,
):
    s = lax.axis_index("seq")
    d = lax.axis_index("dp")
    core = s % 2
    y = (s // 2) % 8
    zl = s // 16
    x = d % 4
    zh = d // 4
    z8 = zh * 4 + zl
    sib = s + 1 - 2 * core

    def at_x(k):
        return {"seq": s, "dp": zh * 4 + (x + k) % 4}

    def at_x_core(xx, cc):
        return {"seq": s - core + cc, "dp": zh * 4 + xx}

    def at_y(yy):
        return {"seq": zl * 16 + yy * 2 + core, "dp": d}

    def at_z(zz):
        return {"seq": (zz % 4) * 16 + y * 2 + core, "dp": (zz // 4) * 4 + x}

    whole = {
        0: edge_s.at[0], 1: edge_s.at[0], 2: stage.at[pl.ds(0, 32)], 6: stage.at[pl.ds(0, 31)], 7: pooled, 12: cot_sib,
        13: b_r1.at[pl.ds(0, 7)], 21: cot_t.at[pl.ds(0, PAD)], 22: cot_t.at[pl.ds(0, PAD)],
        23: t_r1.at[pl.ds(0, 7)], 24: b_r2.at[pl.ds(0, 7)], 28: a_r3.at[pl.ds(0, 7)],
        26: t_r2.at[pl.ds(0, 7)], 27: b_r3.at[pl.ds(0, 3)],
        29: t_r3.at[pl.ds(0, 7)], 31: t_f, 30: a_r4.at[pl.ds(0, 3)],
        3: pfull.at[0, pl.ds(0, 3)], 4: pfull.at[0, pl.ds(0, 4)],
    }
    for h in range(2):
        whole[A_X + h] = a_r1.at[pl.ds(0, 3), pl.ds(0, 2)]
        whole[A_Y + h] = a_r2.at[pl.ds(0, 7), pl.ds(0, 2)]
    for i in range(4):
        whole[Z_PART + i] = pfull.at[0, 0, pl.ds(0, PAD)]
        whole[X_PART + i] = pfull.at[0, pl.ds(0, 3), pl.ds(0, PAD)]
        whole[SIB_PART + i] = pfull.at[0, pl.ds(0, 4), pl.ds(0, PAD)]
    started, ended = [], []
    sibling = {"seq": sib, "dp": d}

    def push(src, dst, i, where):
        if i not in started:
            started.append(i)
        pltpu.make_async_remote_copy(
            src_ref=src, dst_ref=dst, send_sem=send.at[i], recv_sem=recv.at[i],
            device_id=where, device_id_type=MESH,
        ).start()

    def dummy(i):
        ref = whole[i]
        return pltpu.make_async_remote_copy(
            src_ref=ref, dst_ref=ref, send_sem=send.at[i], recv_sem=recv.at[i],
            device_id={"seq": sib, "dp": d}, device_id_type=MESH,
        )

    def arrived(i):
        ended.append(i)
        dummy(i).wait_recv()

    def on_core(c):
        return pl.when(core == c)

    def finish():
        for i in started:
            if i not in ended:
                arrived(i)
            if i == 23:
                for c in range(2):
                    @on_core(c)
                    def _():
                        block = t_r1.at[pl.ds(0, 4 - c)]
                        pltpu.make_async_remote_copy(
                            src_ref=block, dst_ref=block, send_sem=send.at[i], recv_sem=recv.at[i],
                            device_id=sibling, device_id_type=MESH,
                        ).wait_send()
            elif i in (26, 29, 31):
                @on_core(1)
                def _():
                    dummy(i).wait_send()
            elif i in range(Z_PART, Z_PART + 4):
                @pl.when((zl == 0) | (zl == 3))
                def _():
                    dummy(i).wait_send()
                    dummy(i).wait_send()
            else:
                dummy(i).wait_send()

    loads = [
        pltpu.make_async_copy(a, b, load.at[i])
        for i, (a, b) in enumerate(
            (
                (taps_in, taps_ref),
                (dil_in, dil_ref), (link_in, link_ref),
            )
        )
    ]
    barrier = pltpu.get_barrier_semaphore()

    def greet(where):
        pl.semaphore_signal(barrier, inc=1, device_id=where, device_id_type=MESH)

    @pl.loop(1, SEQ)
    def _(k):
        greet({"seq": (s + k) % SEQ, "dp": d})

    for k in range(4):
        greet({"seq": ((zl + k) % 4) * 16 + y * 2 + core, "dp": (1 - zh) * 4 + x})
    for k in range(1, 4):
        greet(at_x(k))
        greet({"seq": sib, "dp": zh * 4 + (x + k) % 4})

    for copy in loads:
        copy.start()

    lane = lax.broadcasted_iota(jnp.int32, (1, HALF), 1)

    def pack_edges(read, dst):
        for side in range(2):
            total = None
            for k in range(8):
                rows = pl.ds(96 * k, 96)
                part = read(1 - side, rows).astype(F32)
                part = pltpu.roll(part, (16 * k + 16 * (1 - side)) % HALF, 1)
                keep = (lane >= 16 * k) & (lane < 16 * k + 16)
                total = jnp.where(keep, part, 0.0 if total is None else total)
            dst[side] = total.astype(BF)

    def halo_keep(width):
        return ((lane < width) & right_linked) | ((lane >= HALF - width) & left_linked)

    def unpack_edges(src, dst):
        from_left = src[0].astype(F32)
        from_right = src[1].astype(F32)
        for k in range(8):
            left = pltpu.roll(from_left, (HALF - 16 - 16 * k) % HALF, 1)
            right = pltpu.roll(from_right, (HALF - 16 * k) % HALF, 1)
            tile = jnp.where(lane < HALF // 2, right, left)
            dst[pl.ds(96 * k, 96), :] = jnp.where(halo_keep(16), tile, 0.0)

    for t in range(SEQ):
        block = cot_ref[0, :, pl.ds(HALF * t, HALF)]
        stage[t] = jnp.concatenate(
            [block.astype(F32), jnp.zeros((PAD - OWN, HALF), F32)], axis=0
        ).astype(BF)

    pack_edges(lambda j, rows: x_ref[0, rows, pl.ds(HALF * j, HALF)], edge_s)

    row = lax.broadcasted_iota(jnp.int32, (64, 112), 0)
    col = lax.broadcasted_iota(jnp.int32, (64, 112), 1)
    inner = row % PAD
    source = OWN * (2 * (row // PAD) + core) + inner
    pick = jnp.where((inner < OWN) & (source == col), 1.0, 0.0).astype(BF)
    pfull[core, d] = jnp.dot(pick, proj_ref[...], preferred_element_type=F32).astype(BF)

    for copy in loads:
        copy.wait()
    left_linked = link_ref[0, s] >= 0
    right_linked = link_ref[0, (s + 1) % SEQ] >= 0
    six = jnp.concatenate([taps_ref[k] for k in range(3)] + [jnp.zeros((2, C), F32)], axis=0)
    six = jnp.transpose(six)
    for i in range(6):
        wide[i] = jnp.broadcast_to(six[:, i:i + 1], (C, HALF))
    d0 = dil_ref[0]


    unit[...] = jnp.where(
        lax.broadcasted_iota(jnp.int32, (HALF, HALF), 0) == lax.broadcasted_iota(jnp.int32, (HALF, HALF), 1),
        1.0, 0.0,
    ).astype(BF)
    two = lax.broadcasted_iota(jnp.int32, (ROWS, HALF), 0) // 2
    pair = two == lax.broadcasted_iota(jnp.int32, (ROWS, HALF), 1)
    halves[...] = jnp.where(pair, 0.5, 0.0).astype(BF)
    ring = 3 * HALF
    shape = (HALF + 2 * PAD, ring)
    at = lax.broadcasted_iota(jnp.int32, shape, 0)
    to = lax.broadcasted_iota(jnp.int32, shape, 1)
    right = (to >= ROWS) & (to < ROWS + 16) & right_linked
    left = (to >= ring - 16) & left_linked
    origin = jnp.where(
        to < ROWS, to // 2,
        jnp.where(right, HALF + (to - ROWS) // 2, jnp.where(left, HALF + 24 + (to - ring + 16) // 2, -1)),
    )
    spread[...] = jnp.where(at == origin, 1.0, 0.0).astype(BF)

    def shifts(dist, length):
        at = lax.broadcasted_iota(jnp.int32, (ring, 2 * length), 0)
        to = lax.broadcasted_iota(jnp.int32, (ring, 2 * length), 1)
        low = to < length
        to = jnp.where(low, to - dist + ring, to - length + dist)
        to = jnp.where(to >= ring, to - ring, to)
        return jnp.where(at == to, 1.0, 0.0).astype(BF)

    matrix1[...] = shifts(LAST_DILATION, ring)
    matrix0[...] = shifts(d0, ROWS)
    which = lax.broadcasted_iota(jnp.int32, (8, 12 * HALF), 1) // HALF
    row = lax.broadcasted_iota(jnp.int32, (8, 12 * HALF), 0)
    pick_taps[...] = jnp.where(which % 6 == row, 1.0, 0.0).astype(BF)

    pl.semaphore_wait(barrier, SEQ - 1 + 4 + 6)

    push(edge_s.at[0], edge_r.at[0], 0, {"seq": (s + 1) % SEQ, "dp": d})
    push(edge_s.at[1], edge_r.at[1], 1, {"seq": (s + SEQ - 1) % SEQ, "dp": d})
    for edge, step in ((0, -1), (3, 1)):
        @pl.when(zl == edge)
        def _():
            for i in range(4):
                rows = pfull.at[core, d, pl.ds(PAD * i, PAD)]
                for far in (2, 1):
                    push(rows, rows, Z_PART + i, at_z((z8 + 8 + far * step) % 8))
    me = core * 32 + zl * 8 + y
    for m in FAR_FIRST:
        t = s ^ m
        push(stage.at[t], cot.at[me], 2 if m & 1 else 6, {"seq": t, "dp": d})

    cot[me] = stage[s]

    for k in (2, 1, 3):
        push(pfull.at[core, d], pfull.at[core, d], 3, at_x(k))
    other = (1 - zh) * 4

    def pass_x(i):
        arrived(Z_PART + i)
        rows = pfull.at[core, other + x, pl.ds(PAD * i, PAD)]
        for k in (2, 1, 3):
            push(rows, rows, X_PART + i, at_x(k))

    def pass_core(i):
        arrived(X_PART + i)
        rows = pfull.at[core, pl.ds(other, 4), pl.ds(PAD * i, PAD)]
        push(rows, rows, SIB_PART + i, sibling)

    def weights(rows):
        return [[wide[2 * k + b, rows, :] for k in range(3)] for b in range(2)]

    @pl.loop(0, C // SLAB)
    def _(i):
        rows = pl.ds(pl.multiple_of(i * SLAB, SLAB), SLAB)
        for j in range(2):
            act, slope = gelu_pair(x_ref[0, rows, HALF * j:HALF * (j + 1)].astype(F32))
            a0[j, rows, :] = act
            s0[j, rows, :] = slope

    arrived(0)
    arrived(1)
    unpack_edges(edge_r, halo)

    def forward(first, last):
        @pl.loop(first, last)
        def _(i):
            rows = pl.ds(pl.multiple_of(i * SLAB, SLAB), SLAB)
            w = weights(rows)
            xs = [x_ref[0, rows, :HALF].astype(F32), x_ref[0, rows, HALF:].astype(F32), halo[rows, :]]
            acts = [a0[0, rows, :], a0[1, rows, :], gelu_pair(xs[2])[0]]
            lo, hi = earlier(acts, lane, d0), later(acts, lane, d0)
            ones = []
            acts1 = []
            for j in range(3):
                v = rounded(xs[j] + ((w[0][0] * lo[j] + w[0][1] * acts[j]) + w[0][2] * hi[j]))
                if j == 2:
                    v = jnp.where(halo_keep(8), v, 0.0)
                ones.append(v)
                act, slope = gelu_pair(v)
                acts1.append(act)
                if j < 2:
                    a1[j, rows, :] = act
                s1[j, rows, :] = slope
            lo, hi = earlier(acts1, lane, LAST_DILATION), later(acts1, lane, LAST_DILATION)
            for j in range(2):
                v = ones[j] + ((w[1][0] * lo[j] + w[1][1] * acts1[j]) + w[1][2] * hi[j])
                x2[rows, HALF * j:HALF * (j + 1)] = v.astype(BF)

    forward(0, 6)
    pass_x(0)
    pass_x(1)
    forward(6, 12)
    pooled[...] = jnp.dot(x2[...], halves[...], preferred_element_type=F32).astype(BF)
    push(pooled, pooled_sib, 7, {"seq": sib, "dp": d})
    pass_x(2)
    pass_x(3)
    arrived(2)
    push(cot.at[pl.ds((1 - core) * 32, 32)], cot_sib, 12, sibling)
    arrived(6)
    nt = (((1,), (1,)), ((), ()))
    cot_t[:HALF] = lax.dot_general(
        unit[...], cot[...].reshape(SEQ * PAD, HALF), nt,
        preferred_element_type=F32,
    ).astype(BF)
    push(cot_t.at[pl.ds(HALF - PAD, PAD)], cot_t.at[pl.ds(HALF + PAD, PAD)], 21, {"seq": (s + 1) % SEQ, "dp": d})
    push(cot_t.at[pl.ds(0, PAD)], cot_t.at[pl.ds(HALF, PAD)], 22, {"seq": (s + SEQ - 1) % SEQ, "dp": d})
    arrived(7)
    arrived(12)
    mine = cot[pl.ds(core * 32, 32)].reshape(512, HALF)
    theirs = cot_sib[...].reshape(512, HALF)
    for j in range(3):
        cols = pl.ds(256 * j, 256)
        part = lax.dot_general(mine, pooled[cols, :], nt, preferred_element_type=F32)
        part = part + lax.dot_general(theirs, pooled_sib[cols, :], nt, preferred_element_type=F32)
        part = part.astype(BF)
        if j == 2:
            b_s1[...] = part.reshape(4, 8, PAD, 256)
            for k in FAR_RING:
                yy = (y + k) % 8
                push(b_s1.at[:, yy], b_r1.at[y], 13, at_y(yy))
        else:
            a_s1[2 * j] = part[:, :HALF].reshape(4, 8, PAD, HALF)
            a_s1[2 * j + 1] = part[:, HALF:].reshape(4, 8, PAD, HALF)
        if j == 1:
            for h in range(2):
                part_z = pl.ds(2 * h, 2)
                for k in (2, 1, 3):
                    push(a_s1.at[(x + k) % 4, part_z], a_r1.at[x, part_z], A_X + h, at_x(k))
    b_r1[y] = b_s1[:, y]
    a_r1[x] = a_s1[x]

    def total(ref):
        parts = [ref[i].astype(F32) for i in range(ref.shape[0])]
        while len(parts) > 1:
            parts = [a + b for a, b in zip(parts[::2], parts[1::2])]
        return parts[0]

    def weight_y(h):
        part_z = pl.ds(2 * h, 2)
        arrived(A_X + h)
        a_s2[part_z] = total(a_r1.at[:, part_z]).astype(BF)
        for k in FAR_RING:
            yy = (y + k) % 8
            push(a_s2.at[part_z, yy], a_r2.at[y, part_z], A_Y + h, at_y(yy))

    arrived(3)
    rows = pfull.at[core, pl.ds(zh * 4, 4)]
    push(rows, rows, 4, sibling)
    for i in range(4):
        pass_core(i)
    for i in (4, SIB_PART, SIB_PART + 1, SIB_PART + 2, SIB_PART + 3, 21, 22):
        arrived(i)
    back = jnp.dot(cot_t[...], pfull[...].reshape(SEQ * PAD, C), preferred_element_type=F32)
    back = (0.5 * back).astype(BF)
    g2[...] = lax.dot_general(
        back, spread[...], (((0,), (0,)), ((), ())), preferred_element_type=F32
    ).astype(BF)

    def keep_product(rows, column, total):
        high = total.astype(BF)
        prods[rows, HALF * column:HALF * (column + 1)] = high
        low = (total - high.astype(F32)).astype(BF)
        prods[rows, HALF * (column + 6):HALF * (column + 7)] = low

    moved[...] = jnp.dot(g2[...], matrix1[...], preferred_element_type=F32)

    @pl.loop(0, C // SLAB)
    def _(i):
        rows = pl.ds(pl.multiple_of(i * SLAB, SLAB), SLAB)
        w = weights(rows)[1]
        g = [g2[rows, HALF * j:HALF * (j + 1)].astype(F32) for j in range(3)]
        lo = [moved[rows, HALF * j:HALF * (j + 1)] for j in range(3)]
        hi = [moved[rows, ring + HALF * j:ring + HALF * (j + 1)] for j in range(3)]
        for j in range(3):
            conv = (w[0] * hi[j] + w[1] * g[j]) + w[2] * lo[j]
            v = g[j] + conv * s1[j, rows, :]
            if j == 2:
                v = jnp.where(halo_keep(8), v, 0.0)
            g1[rows, HALF * j:HALF * (j + 1)] = v.astype(BF)
        for k, part in enumerate((hi, g, lo)):
            keep_product(rows, 2 * k + 1, a1[0, rows, :] * part[0] + a1[1, rows, :] * part[1])

    weight_y(0)
    moved[:, :2 * ROWS] = jnp.dot(g1[...], matrix0[...], preferred_element_type=F32)

    def around(rows):
        g = [g1[rows, HALF * j:HALF * (j + 1)].astype(F32) for j in range(2)]
        lo = [moved[rows, HALF * j:HALF * (j + 1)] for j in range(2)]
        hi = [moved[rows, ROWS + HALF * j:ROWS + HALF * (j + 1)] for j in range(2)]
        return hi, g, lo

    @pl.loop(0, C // SLAB)
    def _(i):
        rows = pl.ds(pl.multiple_of(i * SLAB, SLAB), SLAB)
        for k, part in enumerate(around(rows)):
            keep_product(rows, 2 * k, a0[0, rows, :] * part[0] + a0[1, rows, :] * part[1])

    flat = lax.dot_general(pick_taps[...], prods[...], nt, preferred_element_type=F32)
    slot = x * 2 + core
    t_r1[slot] = jnp.concatenate([flat[:, :384], flat[:, 384:]], axis=0).astype(BF)
    for k in (2, 1, 3):
        push(t_r1.at[slot], t_r1.at[slot], 23, at_x_core((x + k) % 4, 1))

    @on_core(0)
    def _():
        push(t_r1.at[slot], t_r1.at[slot], 23, sibling)

    def push_unless(zz, src):
        @pl.when(zz != z8)
        def _():
            push(src, a_r3.at[z8], 28, at_z(zz))

    weight_y(1)
    a_r2[y] = a_s2[:, y]

    arrived(13)
    b_s2[...] = total(b_r1).astype(BF)
    for k in FAR_RING:
        zz = (z8 + k) % 8
        push(b_s2.at[zz % 4], b_r2.at[z8], 24, at_z(zz))
    b_r2[z8] = b_s2[zl]

    @pl.loop(0, C // SLAB)
    def _(i):
        rows = pl.ds(pl.multiple_of(i * SLAB, SLAB), SLAB)
        w = weights(rows)[0]
        hi, g, lo = around(rows)
        for j in range(2):
            conv = (w[0] * hi[j] + w[1] * g[j]) + w[2] * lo[j]
            out_ref[0, rows, HALF * j:HALF * (j + 1)] = (g[j] + conv * s0[j, rows, :]).astype(BF)

    @on_core(1)
    def _():
        arrived(23)
        t_r2[z8] = total(t_r1).astype(BF)
        for k in FAR_RING:
            push(t_r2.at[z8], t_r2.at[z8], 26, at_z((z8 + k) % 8))

    for h in range(2):
        part_z = pl.ds(2 * h, 2)
        arrived(A_Y + h)
        a_s3[part_z] = total(a_r2.at[:, part_z]).astype(BF)
        for low in (2 * h, 2 * h + 1):
            for high in (0, 4):
                push_unless(high + low, a_s3.at[low])
    a_r3[z8] = a_s3[zl]

    arrived(24)
    b_r3[x] = total(b_r2)
    for k in (1, 3, 2):
        push(b_r3.at[x], b_r3.at[x], 27, at_x(k))

    @on_core(1)
    def _():
        arrived(26)
        t_r3[y] = total(t_r2).astype(BF)
        for k in FAR_RING:
            push(t_r3.at[y], t_r3.at[y], 29, at_y((y + k) % 8))

    arrived(28)
    a_r4[x] = total(a_r3)
    for k in (2, 1, 3):
        push(a_r4.at[x], a_r4.at[x], 30, at_x(k))

    @on_core(1)
    def _():
        arrived(29)
        t_f[...] = total(t_r3)
        push(t_f, t_f, 31, sibling)

    scale = 1.0 / math.sqrt(SEQ * DP * HALF)
    arrived(27)
    pg_ref[:, 512:] = total(b_r3)[:OWN] * scale
    arrived(30)
    for j in range(4):
        pg_ref[:, HALF * j:HALF * (j + 1)] = a_r4[j][:OWN] * scale
    @on_core(0)
    def _():
        arrived(31)

    taps_total = t_f[...]
    for h in range(2):
        for k in range(3):
            tg_ref[k, :, 384 * h:384 * (h + 1)] = taps_total[8 * h + 2 * k:8 * h + 2 * k + 2] * scale

    finish()


def hand_over(*refs):
    sems = refs[6]
    copies = [pltpu.make_async_copy(refs[i], refs[3 + i], sems.at[i]) for i in range(3)]
    for copy in copies:
        copy.start()
    for copy in copies:
        copy.wait()


SCRATCH = [
    ((3, 2, C), F32),
    ((SEQ, PAD, HALF), BF),
    ((SEQ, PAD, HALF), BF),
    ((32, PAD, HALF), BF),
    ((2, DP, 64, C), BF),
    ((2, 96, HALF), BF),
    ((2, 96, HALF), BF),
    ((HALF + 2 * PAD, SEQ * PAD), BF),
    ((C, HALF), F32),
    ((6, C, HALF), F32),
    ((2, C, HALF), F32),
    ((2, C, HALF), F32),
    ((2, C, HALF), F32),
    ((3, C, HALF), F32),
    ((C, ROWS), BF),
    ((C, HALF), BF),
    ((C, HALF), BF),
    ((C, 3 * HALF), BF),
    ((C, 3 * HALF), BF),
    ((C, 6 * HALF), F32),
    ((C, 12 * HALF), BF),
    ((HALF, HALF), BF),
    ((ROWS, HALF), BF),
    ((HALF + 2 * PAD, 3 * HALF), BF),
    ((3 * HALF, 6 * HALF), BF),
    ((3 * HALF, 4 * HALF), BF),
    ((8, 12 * HALF), BF),
    ((4, 4, 8, PAD, HALF), BF),
    ((4, 4, 8, PAD, HALF), BF),
    ((4, 8, PAD, HALF), BF),
    ((8, 4, PAD, HALF), BF),
    ((4, PAD, HALF), BF),
    ((8, PAD, HALF), BF),
    ((4, PAD, HALF), F32),
    ((4, 8, PAD, 256), BF),
    ((8, 4, PAD, 256), BF),
    ((4, PAD, 256), BF),
    ((8, PAD, 256), BF),
    ((4, PAD, 256), F32),
    ((8, PAD, 384), BF),
    ((8, PAD, 384), BF),
    ((8, PAD, 384), BF),
    ((PAD, 384), F32),
]


def local(sequence_acts, taps, dilations, left_link, projection, head_cotangent):
    hbm = pl.BlockSpec(memory_space=pltpu.HBM)
    vmem = pl.BlockSpec(memory_space=pltpu.VMEM)
    results = (
        jax.ShapeDtypeStruct((1, C, ROWS), BF),
        jax.ShapeDtypeStruct((OWN, C), F32),
        jax.ShapeDtypeStruct((3, 2, C), F32),
    )
    parts = pl.pallas_call(
        kernel,
        out_shape=tuple(pltpu.VMEM(r.shape, r.dtype) for r in results),
        in_specs=[vmem, hbm, hbm, hbm, vmem, vmem],
        out_specs=(vmem,) * 3,
        scratch_shapes=[pltpu.VMEM(shape, kind) for shape, kind in SCRATCH[:1]]
        + [pltpu.SMEM((2,), jnp.int32), pltpu.SMEM((1, SEQ), jnp.int32)]
        + [pltpu.VMEM(shape, kind) for shape, kind in SCRATCH[1:]]
        + [pltpu.SemaphoreType.DMA((48,)), pltpu.SemaphoreType.DMA((48,)), pltpu.SemaphoreType.DMA((6,))],
        compiler_params=pltpu.CompilerParams(
            collective_id=0, has_side_effects=True, vmem_limit_bytes=60 * 1024 * 1024
        ),
        cost_estimate=pl.CostEstimate(
            flops=1_000_000_000, bytes_accessed=4_000_000, transcendentals=600_000
        ),
    )(sequence_acts, jnp.transpose(taps, (2, 0, 1)), dilations, left_link, projection, head_cotangent)
    grad, weight, tap_grads = pl.pallas_call(
        hand_over,
        out_shape=results,
        in_specs=[vmem] * 3,
        out_specs=(hbm,) * 3,
        scratch_shapes=[pltpu.SemaphoreType.DMA((3,))],
        compiler_params=pltpu.CompilerParams(vmem_limit_bytes=16 * 1024 * 1024),
    )(*parts)
    return grad, weight, jnp.transpose(tap_grads, (1, 2, 0))


def solution(mesh):
    placed = (P("dp", None, "seq"), P(), P(), P("dp", None), P("dp", None), P("dp", "seq", None))
    return jax.shard_map(
        local,
        mesh=mesh,
        in_specs=placed,
        out_specs=(P("dp", None, "seq"), P("seq", None), P()),
        check_vma=False,
    )
```
